256 devices in a mesh: seq: 32 (over z, x), fsdp: 8 (over y, core).
Axes of the slice: x: 4, y: 4, z: 8, core: 2. Of those that a mesh axis runs over, the one named last changes fastest.
Arguments:
- query_in: bfloat16 [8, 4096, 5120], P('fsdp', 'seq'), may hold values from -400 to 400, as said below
- key_in: bfloat16 [8, 4096, 5120], P('fsdp', 'seq'), may hold values from -400 to 400
- value_in: bfloat16 [8, 4096, 5120], P('fsdp', 'seq'), may hold values from -24 to 24
- out_grad: bfloat16 [8, 4096, 5120], P('fsdp', 'seq'), may hold values from -24 to 24
- gain_q: bfloat16 [5120], P('fsdp'), may hold values from 0.099609375 to 1.8984375
- gain_k: bfloat16 [5120], P('fsdp'), may hold values from 0.099609375 to 1.8984375
- mask_lists: int32 [40, 32, 11], replicated, may hold values from 0 to 31, as said below
- tile_counts: int32 [40, 32], replicated, may hold values from 1 to 11
- head_slot: int32 [40], replicated, may hold values from 0 to 63, as said below
Outputs:
- attn_out: bfloat16 [8, 4096, 5120], P('fsdp', 'seq')
- lse_slots: float32 [8, 64, 4096], P('fsdp', 'seq')
- grad_q: bfloat16 [8, 4096, 5120], P('fsdp', 'seq')
- grad_k: bfloat16 [8, 4096, 5120], P('fsdp', 'seq')
- grad_v: bfloat16 [8, 4096, 5120], P('fsdp', 'seq')
- grad_gain_q: float32 [5120], P('fsdp')
- grad_gain_k: float32 [5120], P('fsdp')
The draws below stay inside these ranges and needn't reach their ends.
Inputs may be any that keep to these rules, and one draw needn't show every extreme that they name: query_in and key_in are finite. `mask_lists`: for head h and query tile i, entries 0 to tile_counts[h, i] - 1 name distinct key tiles in increasing order, tile i among them; the entries after them are ignored. `head_slot`: the 40 heads have distinct slots; slot s belongs to the device of index s // 2 along seq; every device along seq holds between 1 and 2 heads, some device holding 2.
All inputs are finite; a program needn't handle non-finite values.
Results may differ from the reference program's by a relative error of at most 0.035.
The reference program's roundings to bfloat16 on the way count: a program that leaves them out, or rounds other values in their place, can miss the bound.
Values may be sent and summed in bfloat16 or wider, within the bound.
No kernel may reach another device: no remote copies, remote signals or barrier semaphores. Data moves between devices by JAX's collectives and lax.ppermute only.
A program may use at most 128 MiB of HBM per device.

```python
import math
import jax
import jax.numpy as jnp
from jax import lax

H = 40
HD = 128
HW = 5120
TOKENS_CLIP = 4096
NT = 32
TS = 8
TF = 4
RF = 1
RS = 2
KMAX = 11
MAXH = 2
CLIPS = 8
N_SEQ = 32


def window_tables(key):
    key_f, key_s, key_h, key_pad = jax.random.split(key, 4)
    heads_index = jnp.arange(H, dtype=jnp.int32)
    reach_f = jax.random.randint(key_f, (H,), 0, RF + 1)
    reach_s = jax.random.randint(key_s, (H,), 0, RS + 1)
    widest = jax.random.randint(key_h, (), 0, H)
    narrowest = (widest + 1) % H
    reach_f = jnp.where(heads_index == widest, RF, jnp.where(heads_index == narrowest, 0, reach_f))
    reach_s = jnp.where(heads_index == widest, RS, jnp.where(heads_index == narrowest, 0, reach_s))
    tiles_index = jnp.arange(NT, dtype=jnp.int32)
    frame_of = tiles_index // TS
    place_of = tiles_index % TS
    shift_f = jnp.repeat(jnp.arange(-RF, RF + 1, dtype=jnp.int32), 2 * RS + 1)
    shift_s = jnp.tile(jnp.arange(-RS, RS + 1, dtype=jnp.int32), 2 * RF + 1)
    far_corner = (jnp.abs(shift_f) == RF) & (jnp.abs(shift_s) == RS)
    key_frame = frame_of[:, None] + shift_f[None, :]
    key_place = place_of[:, None] + shift_s[None, :]
    inside = (key_frame >= 0) & (key_frame < TF) & (key_place >= 0) & (key_place < TS)
    within = (jnp.abs(shift_f)[None, :] <= reach_f[:, None]) & (jnp.abs(shift_s)[None, :] <= reach_s[:, None]) & jnp.logical_not(far_corner)[None, :]
    usable = inside[None, :, :] & within[:, None, :]
    key_tile = key_frame * TS + key_place
    rank_of = jnp.cumsum(usable.astype(jnp.int32), axis=2) - 1
    counts = jnp.sum(usable.astype(jnp.int32), axis=2)
    positions = jnp.arange(KMAX, dtype=jnp.int32)
    placed = usable[:, :, :, None] & (rank_of[:, :, :, None] == positions[None, None, None, :])
    listed = jnp.sum(jnp.where(placed, key_tile[None, :, :, None], 0), axis=2)
    filler = jax.random.randint(key_pad, (H, NT, KMAX), 0, NT)
    tile_lists = jnp.where(positions[None, None, :] < counts[:, :, None], listed, filler)
    return (tile_lists.astype(jnp.int32), counts.astype(jnp.int32))


def slot_table(key, counts):
    head_load = jnp.sum(counts, axis=1)
    heads_index = jnp.arange(H, dtype=jnp.int32)
    ranking = jnp.argsort(-(head_load * H + heads_index))
    rounds = heads_index // N_SEQ
    column = heads_index % N_SEQ
    before = jnp.where(rounds % 2 == 0, column, N_SEQ - 1 - column)
    shuffled = jax.random.permutation(key, N_SEQ).astype(jnp.int32)
    last_one = N_SEQ - 1
    swapped = jnp.where(shuffled == last_one, shuffled[last_one], shuffled)
    swapped = swapped.at[last_one].set(last_one)
    owner_index = swapped[before]
    slot_by_rank = (owner_index * MAXH + rounds).astype(jnp.int32)
    return jnp.zeros((H,), jnp.int32).at[ranking].set(slot_by_rank)


def query_key(key):
    key_q, key_k = jax.random.split(key, 2)
    array_shape = (CLIPS, TOKENS_CLIP, HW)
    queries = jnp.clip(jax.random.normal(key_q, array_shape, jnp.float32), -4.0, 4.0)
    key_rows = jnp.clip(jax.random.normal(key_k, array_shape, jnp.float32), -4.0, 4.0)
    queries = jnp.clip(queries, -400.0, 400.0)
    key_rows = jnp.clip(key_rows, -400.0, 400.0)
    return (queries.astype(jnp.bfloat16), key_rows.astype(jnp.bfloat16))


def draw_query_in(key, part):
    return query_key(jax.random.fold_in(key, 23))[0]


def draw_key_in(key, part):
    return query_key(jax.random.fold_in(key, 23))[1]


def draw_mask_lists(key, part):
    return window_tables(jax.random.fold_in(key, 11))[0]


def draw_tile_counts(key, part):
    return window_tables(jax.random.fold_in(key, 11))[1]


def draw_head_slot(key, part):
    tile_lists, counts = window_tables(jax.random.fold_in(key, 11))
    return slot_table(jax.random.fold_in(key, 13), counts)


def with_spikes(array, stream_key, source, target, shards_of, factor):
    def block_of(axis_at):
        return (jnp.arange(array.shape[axis_at]) // (array.shape[axis_at] // shards_of)).reshape((-1,) + (1,) * (array.ndim - 1 - axis_at))

    first = jax.random.permutation(stream_key, shards_of)[block_of(target)]
    second = (block_of(target) + shards_of // 2) % shards_of
    return jnp.where((block_of(source) == first) | (block_of(source) == second), factor * array, array)


def shard_levels(key, dims, cuts, low, high):
    def one(dim, blocks):
        steps = jax.random.uniform(jax.random.fold_in(jax.random.fold_in(key, 6), dim), (blocks,), jnp.float32, low / len(cuts), high / len(cuts))
        return jnp.repeat(jnp.exp(steps), dims[dim] // blocks).reshape((-1,) + (1,) * (len(dims) - dim - 1))

    loudness = one(*cuts[0])
    for cut in cuts[1:]:
        loudness = loudness * one(*cut)
    return loudness


def noise(stream_key, dims, spread, reach, cuts=(), kind=jnp.bfloat16):
    gain = shard_levels(stream_key, dims, cuts, -0.22, 0.18) if cuts else 1.0
    array = jax.random.normal(stream_key, dims, jnp.float32) * spread * gain
    return jnp.minimum(jnp.maximum(array, -reach), reach).astype(kind)


def noise_with(stream_key, shape, width, reach, cuts, heavy, kind=jnp.bfloat16):
    values = width * jax.random.normal(stream_key, shape, jnp.float32)
    if cuts:
        values = values * shard_levels(stream_key, shape, cuts, -0.22, 0.18)
    return jnp.clip(with_spikes(values, jax.random.fold_in(stream_key, 3), *heavy), -reach, reach).astype(kind)


def setup_inputs(seed: int = 0) -> dict:
    keys = jax.random.split(jax.random.key(seed), 10)
    return {
        "query_in": draw_query_in(jax.random.fold_in(keys[9], 71), 0),
        "key_in": draw_key_in(jax.random.fold_in(keys[9], 71), 0),
        "value_in": noise(keys[2], (CLIPS, TOKENS_CLIP, HW), 4.0, 24.0, ((0, 8), (1, 32))),
        "out_grad": noise_with(keys[3], (CLIPS, TOKENS_CLIP, HW), 4.0, 24.0, ((0, 8), (1, 32)), (1, 2, 32, 2.75)),
        "gain_q": jnp.clip(1.0 + 0.18 * jax.random.normal(keys[4], (HW,), jnp.float32), 0.099609375, 1.8984375).astype(jnp.bfloat16),
        "gain_k": jnp.clip(1.0 + 0.18 * jax.random.normal(keys[5], (HW,), jnp.float32), 0.099609375, 1.8984375).astype(jnp.bfloat16),
        "mask_lists": draw_mask_lists(jax.random.fold_in(keys[9], 71), 0),
        "tile_counts": draw_tile_counts(jax.random.fold_in(keys[9], 71), 0),
        "head_slot": draw_head_slot(jax.random.fold_in(keys[9], 71), 0),
    }


norm_eps = 1e-06

def normalize(values, gain_vec):
    as_float = values.astype(jnp.float32)
    inverse = lax.rsqrt(lax.optimization_barrier(jnp.mean(as_float * as_float, axis=-1, keepdims=True)) + norm_eps)
    return ((as_float * inverse * gain_vec.astype(jnp.float32)).astype(jnp.bfloat16), inverse)

def norm_backward(values, inverse, gain_vec, upstream):
    as_float = values.astype(jnp.float32)
    incoming = upstream.astype(jnp.float32)
    weighted = incoming * gain_vec.astype(jnp.float32)
    inner_mean = lax.optimization_barrier(jnp.mean(weighted * as_float, axis=-1, keepdims=True))
    grad_in = inverse * weighted - as_float * (inverse * inverse * inverse) * inner_mean
    gain_term = lax.optimization_barrier(jnp.sum(incoming * as_float * inverse, axis=(0, 1)))
    return (grad_in.astype(jnp.bfloat16), gain_term)

def block_group(count_tiles):
    if count_tiles % 4 == 0:
        return 4
    if count_tiles % 2 == 0:
        return 2
    return 1

def masked_scores(query_tiles, key_tiles, counts_blk, score_scale):
    scores = jnp.einsum('gid,gkjd->gikj', query_tiles.astype(jnp.float32), key_tiles.astype(jnp.float32)) * score_scale
    usable = jnp.arange(key_tiles.shape[1], dtype=jnp.int32)[None, :] < counts_blk[:, None]
    return jnp.where(usable[:, None, :, None], scores, -jnp.inf)

def head_forward(query_head, key_head, value_head, tile_lists, counts):
    count_tiles, listed = tile_lists.shape
    head_width = query_head.shape[1]
    tile_rows = query_head.shape[0] // count_tiles
    tile_group = block_group(count_tiles)
    blocks = count_tiles // tile_group
    score_scale = 1.0 / math.sqrt(head_width)
    key_tiles_all = key_head.reshape(count_tiles, tile_rows, head_width)
    value_tiles_all = value_head.reshape(count_tiles, tile_rows, head_width)

    def block_step(pieces):
        query_tiles, lists_blk, counts_blk = pieces
        key_tiles = jnp.take(key_tiles_all, lists_blk, axis=0)
        value_tiles = jnp.take(value_tiles_all, lists_blk, axis=0)
        scores = masked_scores(query_tiles, key_tiles, counts_blk, score_scale)
        row_max = lax.optimization_barrier(jnp.max(scores, axis=(2, 3), keepdims=True))
        row_total = lax.optimization_barrier(jnp.sum(jnp.exp(scores - row_max), axis=(2, 3), keepdims=True))
        log_total = row_max + jnp.log(row_total)
        weights = jnp.exp(scores - log_total).astype(jnp.bfloat16)
        result = jnp.einsum('gikj,gkjd->gid', weights.astype(jnp.float32), value_tiles.astype(jnp.float32))
        return (result.astype(jnp.bfloat16), log_total[:, :, 0, 0])
    result, log_total = lax.map(block_step, (query_head.reshape(blocks, tile_group, tile_rows, head_width), tile_lists.reshape(blocks, tile_group, listed), counts.reshape(blocks, tile_group)))
    return (result.reshape(-1, head_width), log_total.reshape(-1))

def head_backward(query_head, key_head, value_head, result_head, grad_head, log_total, tile_lists, counts):
    count_tiles, listed = tile_lists.shape
    head_width = query_head.shape[1]
    tile_rows = query_head.shape[0] // count_tiles
    tile_group = block_group(count_tiles)
    blocks = count_tiles // tile_group
    score_scale = 1.0 / math.sqrt(head_width)
    key_tiles_all = key_head.reshape(count_tiles, tile_rows, head_width)
    value_tiles_all = value_head.reshape(count_tiles, tile_rows, head_width)

    def shaped(values):
        return values.reshape(blocks, tile_group, tile_rows, head_width)

    def block_step(carried, pieces):
        key_grad, value_grad = carried
        query_tiles, result_tiles, grad_tiles, total_blk, lists_blk, counts_blk = pieces
        key_tiles = jnp.take(key_tiles_all, lists_blk, axis=0)
        value_tiles = jnp.take(value_tiles_all, lists_blk, axis=0)
        scores = masked_scores(query_tiles, key_tiles, counts_blk, score_scale)
        weights = jnp.exp(scores - total_blk[:, :, None, None])
        row_delta = lax.optimization_barrier(jnp.sum(grad_tiles.astype(jnp.float32) * result_tiles.astype(jnp.float32), axis=-1))
        prob_grad = jnp.einsum('gid,gkjd->gikj', grad_tiles.astype(jnp.float32), value_tiles.astype(jnp.float32))
        dscore = (weights * (prob_grad - row_delta[:, :, None, None])).astype(jnp.bfloat16)
        query_grad = jnp.einsum('gikj,gkjd->gid', dscore.astype(jnp.float32), key_tiles.astype(jnp.float32)) * score_scale
        key_part = jnp.einsum('gikj,gid->gkjd', dscore.astype(jnp.float32), query_tiles.astype(jnp.float32)) * score_scale
        value_part = jnp.einsum('gikj,gid->gkjd', weights.astype(jnp.bfloat16).astype(jnp.float32), grad_tiles.astype(jnp.float32))
        key_grad = key_grad.at[lists_blk].add(key_part)
        value_grad = value_grad.at[lists_blk].add(value_part)
        return ((key_grad, value_grad), query_grad.astype(jnp.bfloat16))
    zero_tiles = jnp.zeros((count_tiles, tile_rows, head_width), jnp.float32)
    (key_grad, value_grad), query_grad = lax.scan(block_step, (zero_tiles, zero_tiles), (shaped(query_head), shaped(result_head), shaped(grad_head), log_total.reshape(blocks, tile_group, tile_rows), tile_lists.reshape(blocks, tile_group, listed), counts.reshape(blocks, tile_group)))
    return (query_grad.reshape(-1, head_width), key_grad.reshape(-1, head_width).astype(jnp.bfloat16), value_grad.reshape(-1, head_width).astype(jnp.bfloat16))

def reference(query_in, key_in, value_in, out_grad, gain_q, gain_k, mask_lists, tile_counts, head_slot):
    query_norm, query_inv = normalize(query_in, gain_q)
    key_norm, key_inv = normalize(key_in, gain_k)

    def heads_first(values):
        return values.reshape(CLIPS, TOKENS_CLIP, H, HD).transpose(0, 2, 1, 3).reshape(CLIPS * H, TOKENS_CLIP, HD)

    def heads_back(values):
        return values.reshape(CLIPS, H, TOKENS_CLIP, HD).transpose(0, 2, 1, 3).reshape(CLIPS, TOKENS_CLIP, HW)
    head_ids = jnp.tile(jnp.arange(H, dtype=jnp.int32), CLIPS)

    def per_head(pieces):
        query_head, key_head, value_head, grad_head, head_id = pieces
        tile_lists = mask_lists[head_id]
        counts = tile_counts[head_id]
        result, log_total = head_forward(query_head, key_head, value_head, tile_lists, counts)
        query_grad, key_grad, value_grad = head_backward(query_head, key_head, value_head, result, grad_head, log_total, tile_lists, counts)
        return (result, log_total, query_grad, key_grad, value_grad)
    result, log_total, query_grad, key_grad, value_grad = lax.map(per_head, (heads_first(query_norm), heads_first(key_norm), heads_first(value_in), heads_first(out_grad), head_ids))
    lse_slots = jnp.zeros((CLIPS, N_SEQ * MAXH, TOKENS_CLIP), jnp.float32).at[:, head_slot].set(log_total.reshape(CLIPS, H, TOKENS_CLIP))
    grad_q, term_q = norm_backward(query_in, query_inv, gain_q, heads_back(query_grad))
    grad_k, term_k = norm_backward(key_in, key_inv, gain_k, heads_back(key_grad))
    factor = 1.0 / math.sqrt(CLIPS * TOKENS_CLIP)
    return (heads_back(result), lse_slots, grad_q, grad_k, heads_back(value_grad), term_q * factor, term_k * factor)
```

```python
import functools
import math

import jax
import jax.numpy as jnp
from jax import lax
from jax.experimental import pallas as pl
from jax.experimental.pallas import tpu as pltpu
from jax.sharding import Mesh, PartitionSpec as P

norm_eps = 1e-06
head_width = 128
tile_rows = 128
block = (tile_rows, head_width)
log2e = 1.4426950408889634
ln2 = 0.6931471805599453
masked_out = -1e30
unrolled = 4
vmem_bytes = 26 * 2**20

bf16 = jnp.bfloat16
f32 = jnp.float32
i32 = jnp.int32

vmem = pl.BlockSpec(memory_space=pltpu.VMEM)
smem = pl.BlockSpec(memory_space=pltpu.SMEM)


def dot(a, b, contract):
    dims = ((contract[:1], contract[1:]), ((), ()))
    return lax.dot_general(a, b, dims, preferred_element_type=f32)


def call(kernel, name, outs, in_specs, tiles_moved, flops=0, scratch=(), smem_outs=()):
    out_specs = tuple(smem if n in smem_outs else vmem for n in range(len(outs)))
    return pl.pallas_call(
        kernel,
        out_shape=tuple(jax.ShapeDtypeStruct(*o) for o in outs),
        in_specs=in_specs,
        out_specs=out_specs,
        scratch_shapes=list(scratch),
        compiler_params=pltpu.CompilerParams(vmem_limit_bytes=vmem_bytes),
        cost_estimate=pl.CostEstimate(
            flops=flops, bytes_accessed=tiles_moved * tile_rows * head_width * 2, transcendentals=0
        ),
        name=name,
    )


def cols(head):
    start = head * head_width
    if not isinstance(head, int):
        start = pl.multiple_of(start, head_width)
    return pl.ds(start, head_width)


def place_kernel(n_seq, heads, slot_ref, x_ref, order_ref, main_ref, held_ref):
    @pl.loop(0, 2 * n_seq)
    def _(s):
        held_ref[s] = -1

    @pl.loop(0, heads)
    def _(h):
        held_ref[slot_ref[h]] = h

    def place(position, head):
        order_ref[position] = head
        order_ref[heads + head] = position

    def step(d, used):
        low, high = held_ref[2 * d], held_ref[2 * d + 1]
        place(d, jnp.where(low >= 0, low, high))
        both = jnp.logical_and(low >= 0, high >= 0)

        @pl.when(both)
        def _():
            place(used, high)

        return used + both.astype(i32)

    lax.fori_loop(0, n_seq, step, jnp.int32(n_seq))
    for d in range(n_seq):
        main_ref[d] = x_ref[:, cols(order_ref[d])]


def split_kernel(n_seq, order_ref, x_ref, main_ref):
    for d in range(n_seq):
        main_ref[d] = x_ref[:, cols(order_ref[d])]


def norm_kernel(n_seq, heads, order_ref, q_ref, k_ref, v_ref, do_ref, gain_ref, kq_ref, extra_ref):
    for which, x_ref in ((1, q_ref), (0, k_ref)):
        total = jnp.zeros(block, f32)
        for head in range(heads):
            x = x_ref[:, cols(head)].astype(f32)
            total += x * x
        mean = jnp.sum(total, axis=1, keepdims=True) * (1.0 / (heads * head_width))
        inverse = jnp.broadcast_to(lax.rsqrt(mean + norm_eps), block)
        for p in range(heads):
            at = cols(order_ref[p])
            gain = gain_ref[1 - which : 2 - which, at].astype(f32)
            normed = (x_ref[:, at].astype(f32) * inverse * gain).astype(bf16)
            if p < n_seq:
                kq_ref[p, which] = normed
            else:
                extra_ref[p - n_seq, 2 if which == 0 else 0] = normed
    for p in range(n_seq, heads):
        extra_ref[p - n_seq, 1] = do_ref[:, cols(order_ref[p])]
        extra_ref[p - n_seq, 3] = v_ref[:, cols(order_ref[p])]


def merge_kernel(n_seq, heads, order_ref, main_ref, extra_ref, out_ref, grad_v_ref):
    for p in range(heads):
        at = cols(order_ref[p])
        out_ref[:, at] = main_ref[p, 0] if p < n_seq else extra_ref[p - n_seq, 0]
        grad_v_ref[:, at] = main_ref[p, 1] if p < n_seq else extra_ref[p - n_seq, 3]


def norm_back_kernel(n_seq, heads, order_ref, dqk_ref, extra_ref, q_ref, k_ref, gain_ref, gq_ref, gk_ref):
    scale = 1.0 / (heads * head_width)
    for which, x_ref, out_ref in ((0, q_ref, gq_ref), (1, k_ref, gk_ref)):

        def pieces(p):
            at = cols(order_ref[p])
            up = dqk_ref[p, which] if p < n_seq else extra_ref[p - n_seq, 1 + which]
            gain = gain_ref[which : which + 1, at].astype(f32)
            return at, x_ref[:, at].astype(f32), gain * up.astype(f32)

        squares = jnp.zeros(block, f32)
        inner = jnp.zeros(block, f32)
        for p in range(heads):
            at, x, weighted = pieces(p)
            squares += x * x
            inner += weighted * x
        inverse = lax.rsqrt(jnp.sum(squares, axis=1, keepdims=True) * scale + norm_eps)
        pull = inverse * inverse * inverse * (jnp.sum(inner, axis=1, keepdims=True) * scale)
        inverse = jnp.broadcast_to(inverse, block)
        pull = jnp.broadcast_to(pull, block)
        for p in range(heads):
            at, x, weighted = pieces(p)
            out_ref[:, at] = (inverse * weighted - x * pull).astype(bf16)


def fold_rows(values, combine):
    return combine(values.reshape(values.shape[0] // 8, 8, values.shape[1]), axis=0)


def attention_kernel(parts, most, n_query, n_tiles, group, at, *refs):
    names = ["table", *at["operands"], *at["results"], *at["scratch"]]
    r = dict(zip(names, refs))
    table = r["table"]
    stride = most + 1
    score_scale = log2e / math.sqrt(head_width)
    grad_scale = 1.0 / math.sqrt(head_width)
    key, value, query_of, grad_of = (
        functools.partial(at[k], r) for k in ("key", "value", "query", "grad")
    )
    forward, backward = "forward" in parts, "backward" in parts

    if "prologue" in at:
        at["prologue"](r)
    ahead = at["ahead"]

    @pl.loop(0, n_tiles // unrolled)
    def _(step):
        for t in [step * unrolled + u for u in range(unrolled)]:
            if forward:
                r["dv"][t] = jnp.zeros(block, f32)
            if backward:
                r["dk"][t] = jnp.zeros(block, f32)
            if forward and ahead:
                r["vt"][t] = value(t).T
            if backward and ahead:
                r["kt"][t] = key(t).T

    if backward:
        r["sums"][...] = jnp.zeros(r["sums"].shape, f32)

    def turned(name, t):
        if ahead:
            return r[name][t]
        return (value(t) if name == "vt" else key(t)).T

    def body(count, tiles, counts):
        for a, (i, n) in enumerate(zip(tiles, counts)):
            query, grad = query_of(i), grad_of(i)
            listed = [table[i * stride + j] for j in range(count)]

            def scores(j):
                s = dot(key(listed[j]), query, (1, 1)) * score_scale
                return jnp.where(j < n, s, masked_out) if j else s

            if forward:
                scratch = r["scores"]
                high = None
                for j in range(count):
                    s = scores(j)
                    scratch[a, j] = s
                    peak = fold_rows(s, jnp.max)
                    high = peak if high is None else jnp.maximum(high, peak)
                high = jnp.max(high, axis=0, keepdims=True)
                total = None
                for j in range(count):
                    p = jnp.exp2(scratch[a, j] - high)
                    scratch[a, j] = p
                    part = fold_rows(p, jnp.sum)
                    total = part if total is None else total + part
                total = jnp.sum(total, axis=0, keepdims=True)
                r["lse"][pl.ds(i, 1), :] = high * ln2 + jnp.log(total)
                inverse = 1.0 / total
                probs = [(scratch[a, j] * inverse).astype(bf16) for j in range(count)]
                values_t = jnp.concatenate([turned("vt", t) for t in listed], axis=1)
                out_t = dot(values_t, jnp.concatenate(probs, axis=0), (1, 0)).astype(bf16)
                at["store_out"](r, i, out_t.T)
                delta = jnp.sum(grad.T.astype(f32) * out_t.astype(f32), axis=0, keepdims=True)
                for j, t in enumerate(listed):
                    r["dv"][t] += dot(probs[j], grad, (1, 0))
                if not backward:
                    r["delta"][pl.ds(i, 1), :] = delta
            if backward:
                if not forward:
                    delta = r["delta"][pl.ds(i, 1), :]
                    lse = r["lse"][pl.ds(i, 1), :] * log2e
                dscores = []
                for j, t in enumerate(listed):
                    p = r["scores"][a, j] * inverse if forward else jnp.exp2(scores(j) - lse)
                    dp = dot(value(t), grad, (1, 1))
                    ds = (p * (dp - delta)).astype(bf16)
                    dscores.append(ds)
                    r["dk"][t] += dot(ds, query, (1, 0))
                keys_t = jnp.concatenate([turned("kt", t) for t in listed], axis=1)
                dq_t = dot(keys_t, jnp.concatenate(dscores, axis=0), (1, 0)) * grad_scale
                dq = dq_t.astype(bf16).T
                at["store_dq"](r, i, dq)
                r["sums"][0] += fold_rows(dq.astype(f32) * query.astype(f32), jnp.sum)

    @pl.loop(0, n_query // group)
    def _(g):
        tiles = [g * group + a for a in range(group)]
        counts = [table[t * stride + most] for t in tiles]
        top = functools.reduce(jnp.maximum, counts)
        for static_count in range(1, most + 1):

            @pl.when(top == static_count)
            def _():
                body(static_count, tiles, counts)

    def store_grads(t, where):
        if forward:
            at["store_dv"](r, where, r["dv"][t].astype(bf16))
        if backward:
            dk = (r["dk"][t] * grad_scale).astype(bf16)
            at["store_dk"](r, where, dk)
            r["sums"][1] += fold_rows(dk.astype(f32) * key(t).astype(f32), jnp.sum)

    at["epilogue"](r, store_grads)

    if backward:
        for m in range(2):
            r["gains"][m : m + 1, :] = jnp.sum(r["sums"][m], axis=0, keepdims=True)


def setter(name, where):
    def store(r, i, values):
        r[name][where(i)] = values

    return store


def every_tile(n_tiles, r, store):
    @pl.loop(0, n_tiles // unrolled)
    def _(step):
        for u in range(unrolled):
            store(step * unrolled + u, step * unrolled + u)


def load_shifted(n_x, n_z, r):
    x_index = r["table"][r["table"].shape[0] - 1]
    for s in range(n_x):
        x = lax.rem(x_index + n_x - s, n_x)
        source = r["own"] if s == 0 else r[f"kv{s}"]
        for z in range(n_z):
            for m in range(2):
                r["kv"][z * n_x + x, m] = source[z, 2 + m] if s == 0 else source[z, m]


def store_shifted(n_x, n_z, r, store):
    x_index = r["table"][r["table"].shape[0] - 1]
    for s in range(n_x):
        x = lax.rem(x_index + s, n_x)

        @pl.loop(0, n_z)
        def _(z):
            store(z * n_x + x, (s, z))


def store_part(m):
    def store(r, where, values):
        s, z = where
        r[f"part{s}"][z, m] = values

    return store


def collect_kernel(odq_ref, *refs):
    parts, back_ref = refs[:-1], refs[-1]

    @pl.loop(0, back_ref.shape[0])
    def _(z):
        for m in range(2):
            back_ref[z, m] = odq_ref[z, m]
            total = sum(part[z, m].astype(f32) for part in parts)
            back_ref[z, 2 + m] = total.astype(bf16)


def finish_kernel(n_x, n_z, heads, per, order_ref, slot_ref, here_ref, lse_ref, shared_ref, gq_ref, gk_ref, out_ref, sq_ref, sk_ref):
    n_seq = n_x * n_z
    own, f_index = here_ref[0], here_ref[1]
    out_ref[...] = jnp.zeros(out_ref.shape, f32)
    out_ref[lax.rem(slot_ref[order_ref[own]], 2)] = lse_ref[...]

    @pl.loop(0, heads - n_seq)
    def _(e):
        slot = slot_ref[order_ref[n_seq + e]]

        @pl.when(lax.div(slot, 2) == own)
        def _():
            for x in range(n_x):
                for z in range(n_z):
                    row = z * n_x + x
                    out_ref[lax.rem(slot, 2), row : row + 1, :] = shared_ref[e * n_x + x, z : z + 1, :]

    factor = 1.0 / math.sqrt(n_seq * tile_rows * (heads // per))
    for j in range(per):
        position = order_ref[heads + f_index * per + j]
        for m, (gain_ref, out) in enumerate(((gq_ref, sq_ref), (gk_ref, sk_ref))):
            first = shared_ref[jnp.minimum(position, n_seq - 1), n_z + m : n_z + m + 1, :]
            spread = jnp.maximum(position - n_seq, 0) * n_x
            second = sum(shared_ref[spread + x, n_z + 2 + m : n_z + 3 + m, :] for x in range(n_x))
            total = jnp.where(position < n_seq, first, second)
            out[j : j + 1, :] = total / gain_ref[j : j + 1, :].astype(f32) * factor


def after(values, done):
    return lax.optimization_barrier((values, done))[0]


def shards(query_in, key_in, value_in, out_grad, gain_q, gain_k, mask_lists, tile_counts, head_slot):
    n_x, n_z, n_f = lax.axis_size("x"), lax.axis_size("z"), lax.axis_size("fsdp")
    n_seq = n_x * n_z
    x_index, z_index, f_index = lax.axis_index("x"), lax.axis_index("z"), lax.axis_index("fsdp")
    own = z_index * n_x + x_index
    heads, n_tiles, most = mask_lists.shape
    extra = heads - n_seq
    features = heads * head_width
    seq_axes = ("z", "x")
    q2, k2, v2, g2 = (a.reshape(tile_rows, features) for a in (query_in, key_in, value_in, out_grad))

    def swap(values, axes):
        return lax.all_to_all(values, axes, split_axis=0, concat_axis=0, tiled=True)

    order, value_send = call(
        functools.partial(place_kernel, n_seq, heads),
        "place_heads",
        [((2 * heads,), i32), ((n_seq, *block), bf16)],
        [smem, vmem],
        2 * heads,
        scratch=[pltpu.SMEM((2 * n_seq,), i32)],
        smem_outs=(0,),
    )(head_slot, v2)
    value_main = swap(value_send, seq_axes)

    gains = lax.all_gather(jnp.stack([gain_q, gain_k]), "fsdp", axis=1, tiled=True)
    kq_send, extra_send = call(
        functools.partial(norm_kernel, n_seq, heads),
        "normalize",
        [((n_seq, 2, *block), bf16), ((extra, 4, *block), bf16)],
        [smem] + [vmem] * 5,
        6 * heads,
    )(order, q2, k2, v2, g2, gains)
    extra_own = swap(after(extra_send, value_main), "z")
    (grad_send,) = call(
        functools.partial(split_kernel, n_seq),
        "split_heads",
        [((n_seq, *block), bf16)],
        [smem, vmem],
        2 * heads,
    )(order, g2)
    grad_main = swap(after(grad_send, extra_own), seq_axes)

    table = jnp.concatenate([mask_lists, tile_counts[:, :, None]], axis=2)
    table_main = lax.dynamic_index_in_dim(table, order[own], 0, keepdims=False).reshape(-1)
    table_extra = lax.dynamic_index_in_dim(table, order[n_seq + z_index], 0, keepdims=False)
    table_extra = lax.dynamic_index_in_dim(
        table_extra.reshape(n_z, n_x, most + 1), x_index, 1, keepdims=False
    )
    table_extra = jnp.concatenate([table_extra.reshape(-1), x_index[None]])

    def attention(parts, name, n_query, at, outs, n_operands, passes):
        group = 2
        tile_f32 = pltpu.VMEM((n_tiles, *block), f32)
        tile_bf16 = pltpu.VMEM((n_tiles, *block), bf16)
        scratch = {}
        if "forward" in parts:
            scratch |= {"vt": tile_bf16, "dv": tile_f32, "scores": pltpu.VMEM((group, most, *block), f32)}
        if "backward" in parts:
            scratch |= {"kt": tile_bf16, "dk": tile_f32, "sums": pltpu.VMEM((2, 8, head_width), f32)}
        if not at["ahead"]:
            scratch = {n: v for n, v in scratch.items() if n not in ("kt", "vt")}
            scratch["kv"] = pltpu.VMEM((n_tiles, 2, *block), bf16)
        at = {**at, "scratch": list(scratch), "results": list(outs)}
        return call(
            functools.partial(attention_kernel, parts, most, n_query, n_tiles, group, at),
            name,
            list(outs.values()),
            [smem] + [vmem] * n_operands,
            10 * n_tiles,
            flops=n_query * most * passes * 2 * tile_rows * tile_rows * head_width,
            scratch=list(scratch.values()),
        )

    rows_of = lambda n: ((n, tile_rows), f32)

    def shift(values, s):
        return lax.ppermute(values, "x", [(x, (x + s) % n_x) for x in range(n_x)])

    kv_own = extra_own[:, 2:4]
    kv_shifted = [shift(kv_own, s) for s in range(1, n_x)]
    kq_main = swap(after(kq_send, (grad_main, kv_shifted)), seq_axes)
    kv_shifted = after(kv_shifted, grad_main)
    odq_extra, lse_extra, gain_extra, *dkv_parts = attention(
        ("forward", "backward"),
        "attention_second",
        n_z,
        {
            "operands": ["own", *(f"kv{s}" for s in range(1, n_x))],
            "key": lambda r, t: r["kv"][t, 0],
            "value": lambda r, t: r["kv"][t, 1],
            "query": lambda r, i: r["own"][i, 0],
            "grad": lambda r, i: r["own"][i, 1],
            "ahead": False,
            "prologue": functools.partial(load_shifted, n_x, n_z),
            "epilogue": functools.partial(store_shifted, n_x, n_z),
            "store_out": setter("odq", lambda i: (i, 0)),
            "store_dq": setter("odq", lambda i: (i, 1)),
            "store_dk": store_part(0),
            "store_dv": store_part(1),
        },
        {
            "odq": ((n_z, 2, *block), bf16),
            "lse": rows_of(n_z),
            "gains": ((2, head_width), f32),
            **{f"part{s}": ((n_z, 2, *block), bf16) for s in range(n_x)},
        },
        n_x,
        20,
    )(table_extra, extra_own, *kv_shifted)
    dkv_parts = [dkv_parts[0], *(shift(dkv_parts[s], s) for s in range(1, n_x))]
    (extra_back,) = call(
        collect_kernel, "collect", [((n_z, 4, *block), bf16)], [vmem] * (1 + n_x), 8 * n_z
    )(odq_extra, *dkv_parts)
    extra_home = swap(after(extra_back, kq_main), "z")

    main_at = {
        "ahead": True,
        "epilogue": functools.partial(every_tile, n_tiles),
        "key": lambda r, t: r["kq"][t, 0],
        "value": lambda r, t: r["v"][t],
        "query": lambda r, i: r["kq"][i, 1],
        "grad": lambda r, i: r["g"][i],
    }
    odv_main, lse_main, delta_main = attention(
        ("forward",),
        "forward_first",
        n_tiles,
        {
            **main_at,
            "operands": ["kq", "v", "g"],
            "store_out": setter("odv", lambda i: (i, 0)),
            "store_dv": setter("odv", lambda t: (t, 1)),
        },
        {"odv": ((n_tiles, 2, *block), bf16), "lse": rows_of(n_tiles), "delta": rows_of(n_tiles)},
        3,
        10,
    )(table_main, kq_main, value_main, grad_main)
    odv_home = swap(after(odv_main, extra_home), seq_axes)
    dqk_main, gain_main = attention(
        ("backward",),
        "backward_first",
        n_tiles,
        {
            **main_at,
            "operands": ["kq", "v", "g", "lse", "delta"],
            "store_dq": setter("dqk", lambda i: (i, 0)),
            "store_dk": setter("dqk", lambda t: (t, 1)),
        },
        {"dqk": ((n_tiles, 2, *block), bf16), "gains": ((2, head_width), f32)},
        5,
        16,
    )(table_main, kq_main, value_main, grad_main, lse_main, delta_main)
    dqk_home = swap(after(dqk_main, odv_home), seq_axes)

    wide = ((tile_rows, features), bf16)
    attn_out, grad_v = call(
        functools.partial(merge_kernel, n_seq, heads),
        "merge_heads",
        [wide, wide],
        [smem, vmem, vmem],
        4 * heads,
    )(order, odv_home, extra_home)
    grad_q, grad_k = call(
        functools.partial(norm_back_kernel, n_seq, heads),
        "normalize_back",
        [wide, wide],
        [smem] + [vmem] * 5,
        6 * heads,
    )(order, dqk_home, extra_home, q2, k2, gains)

    gain_sums = lax.psum(jnp.concatenate([gain_main, gain_extra]), "fsdp")
    shared = jnp.concatenate([lse_extra, gain_sums, jnp.zeros((4, head_width), f32)])
    shared = lax.all_gather(lax.all_gather(shared, "x", axis=0), "z", axis=0)
    shared = shared.reshape(n_seq, -1, head_width)
    per = heads // n_f
    lse_slots, share_q, share_k = call(
        functools.partial(finish_kernel, n_x, n_z, heads, per),
        "finish",
        [((2, n_tiles, tile_rows), f32), ((per, head_width), f32), ((per, head_width), f32)],
        [smem] * 3 + [vmem] * 4,
        32,
    )(
        order,
        head_slot,
        jnp.stack([own, f_index]),
        lse_main,
        shared,
        gain_q.reshape(per, head_width),
        gain_k.reshape(per, head_width),
    )
    whole = lambda a: a.reshape(1, tile_rows, features)
    return (
        whole(attn_out),
        lse_slots.reshape(1, 2, n_tiles * tile_rows),
        whole(grad_q),
        whole(grad_k),
        whole(grad_v),
        share_q.reshape(-1),
        share_k.reshape(-1),
    )


def solution(mesh):
    n_seq, n_f = mesh.devices.shape
    n_z = 8
    grid = Mesh(mesh.devices.reshape(n_z, n_seq // n_z, n_f), ("z", "x", "fsdp"))
    rows = P("fsdp", ("z", "x"), None)
    in_specs = (rows,) * 4 + (P("fsdp"),) * 2 + (P(),) * 3
    out_specs = (rows,) * 5 + (P("fsdp"),) * 2
    return jax.shard_map(shards, mesh=grid, in_specs=in_specs, out_specs=out_specs, check_vma=False)
```

```python
import functools
import math

import jax
import jax.numpy as jnp
from jax import lax
from jax.experimental import pallas as pl
from jax.experimental.pallas import tpu as pltpu
from jax.sharding import Mesh, PartitionSpec as P

norm_eps = 1e-06
head_width = 128
tile_rows = 128
block = (tile_rows, head_width)
log2e = 1.4426950408889634
ln2 = 0.6931471805599453
masked_out = -1e30
unrolled = 4
vmem_bytes = 26 * 2**20
most_vmem = 60 * 2**20

bf16 = jnp.bfloat16
f32 = jnp.float32
i32 = jnp.int32

vmem = pl.BlockSpec(memory_space=pltpu.VMEM)
smem = pl.BlockSpec(memory_space=pltpu.SMEM)
hbm = pl.BlockSpec(memory_space=pltpu.HBM)


def dot(a, b, contract):
    dims = ((contract[:1], contract[1:]), ((), ()))
    return lax.dot_general(a, b, dims, preferred_element_type=f32)


def staged(kernel, n_in, n_out, hbm_in, hbm_out, lazy, refs):
    ins, outs = list(refs[:n_in]), list(refs[n_in : n_in + n_out])
    rest = refs[n_in + n_out :]
    n_hbm = len(hbm_in) + len(hbm_out)
    scratch, buffers, sems = rest[: len(rest) - n_hbm - 1], rest[len(rest) - n_hbm - 1 : -1], rest[-1]
    reads, writes = {}, {}
    for c, i in enumerate(hbm_in):
        reads[i] = pltpu.make_async_copy(ins[i], buffers[c], sems.at[c])
        reads[i].start()
        ins[i] = buffers[c]
    for c, o in enumerate(hbm_out, len(hbm_in)):
        writes[o] = pltpu.make_async_copy(buffers[c], outs[o], sems.at[c])
        outs[o] = buffers[c]
    if lazy:
        kernel(*ins, *outs, *scratch, ready=lambda i: reads[i].wait(), flush=lambda o: writes[o].start())
    else:
        for i in hbm_in:
            reads[i].wait()
        kernel(*ins, *outs, *scratch)
        for o in hbm_out:
            writes[o].start()
    for o in hbm_out:
        writes[o].wait()


def call(kernel, name, outs, in_specs, tiles_moved, flops=0, scratch=(), smem_outs=(), hbm_in=(), hbm_out=(), lazy=False, room=vmem_bytes):
    def run(*operands):
        specs = [hbm if i in hbm_in else spec for i, spec in enumerate(in_specs)]
        kinds = (smem if n in smem_outs else hbm if n in hbm_out else vmem for n in range(len(outs)))
        buffers = [pltpu.VMEM(operands[i].shape, operands[i].dtype) for i in hbm_in]
        buffers += [pltpu.VMEM(*outs[o]) for o in hbm_out]
        body, extra = kernel, []
        if buffers:
            body = lambda *refs: staged(kernel, len(specs), len(outs), hbm_in, hbm_out, lazy, refs)
            extra = [*buffers, pltpu.SemaphoreType.DMA((len(buffers),))]
        return pl.pallas_call(
            body,
            out_shape=tuple(jax.ShapeDtypeStruct(*o) for o in outs),
            in_specs=specs,
            out_specs=tuple(kinds),
            scratch_shapes=[*scratch, *extra],
            compiler_params=pltpu.CompilerParams(
                vmem_limit_bytes=most_vmem if buffers else room
            ),
            cost_estimate=pl.CostEstimate(
                flops=flops, bytes_accessed=tiles_moved * tile_rows * head_width * 2, transcendentals=0
            ),
            name=name,
        )(*operands)

    return run


def cols(head):
    start = head * head_width
    if not isinstance(head, int):
        start = pl.multiple_of(start, head_width)
    return pl.ds(start, head_width)


def place_kernel(n_seq, heads, slot_ref, x_hbm, order_ref, main_hbm, held_ref, x_ref, read_sem, write_sems):
    read = pltpu.make_async_copy(x_hbm, x_ref, read_sem)
    read.start()

    @pl.loop(0, 2 * n_seq)
    def _(s):
        held_ref[s] = -1

    @pl.loop(0, heads)
    def _(h):
        held_ref[slot_ref[h]] = h

    def place(position, head):
        order_ref[position] = head
        order_ref[heads + head] = position

    def step(d, used):
        low, high = held_ref[2 * d], held_ref[2 * d + 1]
        place(d, jnp.where(low >= 0, low, high))
        both = jnp.logical_and(low >= 0, high >= 0)

        @pl.when(both)
        def _():
            place(used, high)

        return used + both.astype(i32)

    lax.fori_loop(0, n_seq, step, jnp.int32(n_seq))
    read.wait()
    writes = [
        pltpu.make_async_copy(x_ref.at[:, cols(order_ref[d])], main_hbm.at[d], write_sems.at[d])
        for d in range(n_seq)
    ]
    for write in writes:
        write.start()
    for write in writes:
        write.wait()


def norm_kernel(n_seq, heads, order_ref, q_ref, k_ref, v_ref, do_ref, gain_ref, kq_ref, grad_ref, extra_ref):
    for p in range(n_seq):
        grad_ref[p] = do_ref[:, cols(order_ref[p])]
    for which, x_ref in ((1, q_ref), (0, k_ref)):
        total = jnp.zeros(block, f32)
        for head in range(heads):
            x = x_ref[:, cols(head)].astype(f32)
            total += x * x
        mean = jnp.sum(total, axis=1, keepdims=True) * (1.0 / (heads * head_width))
        inverse = jnp.broadcast_to(lax.rsqrt(mean + norm_eps), block)
        for p in range(heads):
            at = cols(order_ref[p])
            gain = gain_ref[1 - which : 2 - which, at].astype(f32)
            normed = (x_ref[:, at].astype(f32) * inverse * gain).astype(bf16)
            if p < n_seq:
                kq_ref[p, which] = normed
            else:
                extra_ref[p - n_seq, 2 if which == 0 else 0] = normed
    for p in range(n_seq, heads):
        extra_ref[p - n_seq, 1] = do_ref[:, cols(order_ref[p])]
        extra_ref[p - n_seq, 3] = v_ref[:, cols(order_ref[p])]


def merge_kernel(n_seq, heads, order_ref, main_ref, extra_ref, out_ref, grad_v_ref):
    for p in range(heads):
        at = cols(order_ref[p])
        out_ref[:, at] = main_ref[p, 0] if p < n_seq else extra_ref[p - n_seq, 0]
        grad_v_ref[:, at] = main_ref[p, 1] if p < n_seq else extra_ref[p - n_seq, 3]


def back_kernel(n_seq, heads, order_ref, main_ref, extra_ref, q_ref, k_ref, gain_ref, gq_ref, gk_ref, ready, flush):
    ready(2)
    ready(1)
    scale = 1.0 / (heads * head_width)
    for which, x_ref, out_ref in ((0, q_ref, gq_ref), (1, k_ref, gk_ref)):
        ready(3 + which)

        def pieces(p):
            at = cols(order_ref[p])
            up = main_ref[p, pl.ds(which * tile_rows, tile_rows)] if p < n_seq else extra_ref[p - n_seq, 1 + which]
            gain = gain_ref[which : which + 1, at].astype(f32)
            return at, x_ref[:, at].astype(f32), gain * up.astype(f32)

        squares = jnp.zeros(block, f32)
        inner = jnp.zeros(block, f32)
        for p in range(heads):
            at, x, weighted = pieces(p)
            squares += x * x
            inner += weighted * x
        inverse = lax.rsqrt(jnp.sum(squares, axis=1, keepdims=True) * scale + norm_eps)
        pull = inverse * inverse * inverse * (jnp.sum(inner, axis=1, keepdims=True) * scale)
        inverse = jnp.broadcast_to(inverse, block)
        pull = jnp.broadcast_to(pull, block)
        for p in range(heads):
            at, x, weighted = pieces(p)
            out_ref[:, at] = (inverse * weighted - x * pull).astype(bf16)
        flush(which)


def fold_rows(values, combine):
    return combine(values.reshape(values.shape[0] // 8, 8, values.shape[1]), axis=0)


def attention_kernel(parts, most, n_query, n_tiles, group, at, *refs):
    names = ["table", *at["operands"], *at["results"], *at["scratch"]]
    r = dict(zip(names, refs))
    table = r["table"]
    stride = most + 1
    score_scale = log2e / math.sqrt(head_width)
    grad_scale = 1.0 / math.sqrt(head_width)
    key, value, query_of, grad_of = (
        functools.partial(at[k], r) for k in ("key", "value", "query", "grad")
    )
    forward, backward = "forward" in parts, "backward" in parts

    if "prologue" in at:
        at["prologue"](r)
    ahead = at["ahead"]

    @pl.loop(0, n_tiles // unrolled)
    def _(step):
        for t in [step * unrolled + u for u in range(unrolled)]:
            if forward:
                r["dv"][t] = jnp.zeros(block, f32)
            if backward:
                r["dk"][t] = jnp.zeros(block, f32)
            if forward and ahead:
                r["vt"][t] = value(t).T
            if backward and ahead:
                r["kt"][t] = key(t).T

    if backward:
        r["sums"][...] = jnp.zeros(r["sums"].shape, f32)

    def turned(name, t):
        if ahead:
            return r[name][t]
        return (value(t) if name == "vt" else key(t)).T

    def body(count, tiles, counts):
        for a, (i, n) in enumerate(zip(tiles, counts)):
            query, grad = query_of(i), grad_of(i)
            listed = [table[i * stride + j] for j in range(count)]

            def scores(j):
                s = dot(key(listed[j]), query, (1, 1)) * score_scale
                return jnp.where(j < n, s, masked_out) if j else s

            if forward:
                scratch = r["scores"]
                high = None
                for j in range(count):
                    s = scores(j)
                    scratch[a, j] = s
                    peak = fold_rows(s, jnp.max)
                    high = peak if high is None else jnp.maximum(high, peak)
                high = jnp.max(high, axis=0, keepdims=True)
                total = None
                for j in range(count):
                    p = jnp.exp2(scratch[a, j] - high)
                    scratch[a, j] = p
                    part = fold_rows(p, jnp.sum)
                    total = part if total is None else total + part
                total = jnp.sum(total, axis=0, keepdims=True)
                r["lse"][pl.ds(i, 1), :] = high * ln2 + jnp.log(total)
                inverse = 1.0 / total
                probs = [(scratch[a, j] * inverse).astype(bf16) for j in range(count)]
                values_t = jnp.concatenate([turned("vt", t) for t in listed], axis=1)
                out_t = dot(values_t, jnp.concatenate(probs, axis=0), (1, 0)).astype(bf16)
                at["store_out"](r, i, out_t.T)
                delta = jnp.sum(grad.T.astype(f32) * out_t.astype(f32), axis=0, keepdims=True)
                for j, t in enumerate(listed):
                    r["dv"][t] += dot(probs[j], grad, (1, 0))
                if not backward:
                    r["delta"][pl.ds(i, 1), :] = delta
            if backward:
                if not forward:
                    delta = r["delta"][pl.ds(i, 1), :]
                    lse = r["lse"][pl.ds(i, 1), :] * log2e
                if not forward:
                    for j in range(count):
                        r["scores"][a, j] = scores(j)
                for j, t in enumerate(listed):
                    r["dprobs"][a, j] = dot(value(t), grad, (1, 1))
                dscores = []
                for j in range(count):
                    s = r["scores"][a, j]
                    p = s * inverse if forward else jnp.exp2(s - lse)
                    dscores.append((p * (r["dprobs"][a, j] - delta)).astype(bf16))
                for j, t in enumerate(listed):
                    r["dk"][t] += dot(dscores[j], query, (1, 0))
                keys_t = jnp.concatenate([turned("kt", t) for t in listed], axis=1)
                dq_t = dot(keys_t, jnp.concatenate(dscores, axis=0), (1, 0)) * grad_scale
                dq = dq_t.astype(bf16).T
                at["store_dq"](r, i, dq)
                r["sums"][0] += fold_rows(dq.astype(f32) * query.astype(f32), jnp.sum)

    @pl.loop(0, n_query // group)
    def _(g):
        tiles = [g * group + a for a in range(group)]
        counts = [table[t * stride + most] for t in tiles]
        top = functools.reduce(jnp.maximum, counts)
        for static_count in range(1, most + 1):

            @pl.when(top == static_count)
            def _():
                body(static_count, tiles, counts)

    def store_grads(t, where):
        if forward:
            at["store_dv"](r, where, r["dv"][t].astype(bf16))
        if backward:
            dk = (r["dk"][t] * grad_scale).astype(bf16)
            at["store_dk"](r, where, dk)
            r["sums"][1] += fold_rows(dk.astype(f32) * key(t).astype(f32), jnp.sum)

    at["epilogue"](r, store_grads)

    if backward:
        for m in range(2):
            r["gains"][m : m + 1, :] = jnp.sum(r["sums"][m], axis=0, keepdims=True)


def setter(name, where):
    def store(r, i, values):
        r[name][where(i)] = values

    return store


def store_dk_first(r, t, values):
    r["dqk"][t, pl.ds(tile_rows, tile_rows)] = values
    r["dqk"][t, pl.ds(2 * tile_rows, shared_rows)] = jnp.zeros((shared_rows, head_width), bf16)


def every_tile(n_tiles, r, store):
    @pl.loop(0, n_tiles // unrolled)
    def _(step):
        for u in range(unrolled):
            store(step * unrolled + u, step * unrolled + u)


def load_shifted(n_x, n_z, r):
    x_index = r["table"][r["table"].shape[0] - 1]
    for s in range(n_x):
        x = lax.rem(x_index + n_x - s, n_x)
        source = r["own"] if s == 0 else r[f"kv{s}"]
        for z in range(n_z):
            for m in range(2):
                r["kv"][z * n_x + x, m] = source[z, 2 + m] if s == 0 else source[z, m]


def store_shifted(n_x, n_z, r, store):
    x_index = r["table"][r["table"].shape[0] - 1]
    for s in range(n_x):
        x = lax.rem(x_index + s, n_x)

        @pl.loop(0, n_z)
        def _(z):
            store(z * n_x + x, (s, z))


def store_part(m):
    def store(r, where, values):
        s, z = where
        r[f"part{s}"][z, m] = values

    return store


def add_kernel(one_ref, two_ref, sum_ref):
    @pl.loop(0, sum_ref.shape[0])
    def _(z):
        sum_ref[z] = (one_ref[z].astype(f32) + two_ref[z].astype(f32)).astype(bf16)


def collect_kernel(odq_ref, *refs):
    parts, back_ref = refs[:-1], refs[-1]

    @pl.loop(0, back_ref.shape[0])
    def _(z):
        for m in range(2):
            back_ref[z, m] = odq_ref[z, m]
            total = sum(part[z, m].astype(f32) for part in parts)
            back_ref[z, 2 + m] = total.astype(bf16)


shared_rows = 32


def share_kernel(sums_ref, lse_ref, unused_hbm, back_hbm, terms_ref, rows_ref, sems):
    value = sums_ref[...]
    for term in range(2):
        part = value.astype(bf16).astype(f32)
        terms_ref[4 * term : 4 * term + 4, :] = part
        value = value - part
    value = lse_ref[...]
    for term in range(1, 4):
        part = value.astype(bf16).astype(f32)
        terms_ref[8 * term : 8 * term + 8, :] = part
        value = value - part
    rows_ref[...] = terms_ref[...].astype(bf16)
    n_seq, n_rows = back_hbm.shape[:2]
    last = pl.ds(n_rows - shared_rows, shared_rows)
    copies = [pltpu.make_async_copy(rows_ref, back_hbm.at[d, last], sems.at[d]) for d in range(n_seq)]
    for copy in copies:
        copy.start()
    for copy in copies:
        copy.wait()


def finish_kernel(n_x, n_z, heads, per, order_ref, slot_ref, here_ref, lse_ref, gq_ref, gk_ref, home_hbm, out_ref, sq_ref, sk_ref, rows_ref, shared_ref, sem):
    n_seq = n_x * n_z
    own, f_index = here_ref[0], here_ref[1]
    last = pl.ds(home_hbm.shape[1] - shared_rows, shared_rows)
    copy = pltpu.make_async_copy(home_hbm.at[:, last], rows_ref, sem)
    copy.start()
    copy.wait()
    shared_ref[...] = rows_ref[...].astype(f32)

    def row(device, line):
        lines = [8 * t + line for t in range(1, 4)] if line < n_z else [line - n_z, line - n_z + 4]
        return sum(shared_ref[device, n : n + 1, :] for n in lines)

    out_ref[...] = jnp.zeros(out_ref.shape, f32)
    out_ref[lax.rem(slot_ref[order_ref[own]], 2)] = lse_ref[...]

    @pl.loop(0, heads - n_seq)
    def _(e):
        slot = slot_ref[order_ref[n_seq + e]]

        @pl.when(lax.div(slot, 2) == own)
        def _():
            for x in range(n_x):
                for z in range(n_z):
                    at = z * n_x + x
                    out_ref[lax.rem(slot, 2), at : at + 1, :] = row(e * n_x + x, z)

    factor = 1.0 / math.sqrt(n_seq * tile_rows * (heads // per))
    for j in range(per):
        position = order_ref[heads + f_index * per + j]
        for m, (gain_ref, out) in enumerate(((gq_ref, sq_ref), (gk_ref, sk_ref))):
            first = row(jnp.minimum(position, n_seq - 1), n_z + m)
            spread = jnp.maximum(position - n_seq, 0) * n_x
            second = sum(row(spread + x, n_z + 2 + m) for x in range(n_x))
            total = jnp.where(position < n_seq, first, second)
            out[j : j + 1, :] = total / gain_ref[j : j + 1, :].astype(f32) * factor


def after(values, done):
    return lax.optimization_barrier((values, done))[0]


def shards(query_in, key_in, value_in, out_grad, gain_q, gain_k, mask_lists, tile_counts, head_slot):
    n_x, n_z, n_f = lax.axis_size("x"), lax.axis_size("z"), lax.axis_size("fsdp")
    n_seq = n_x * n_z
    x_index, z_index, f_index = lax.axis_index("x"), lax.axis_index("z"), lax.axis_index("fsdp")
    own = z_index * n_x + x_index
    heads, n_tiles, most = mask_lists.shape
    extra = heads - n_seq
    features = heads * head_width
    seq_axes = ("z", "x")
    q2, k2, v2, g2 = (a.reshape(tile_rows, features) for a in (query_in, key_in, value_in, out_grad))

    def swap(values, axes):
        return lax.all_to_all(values, axes, split_axis=0, concat_axis=0, tiled=True)

    order, value_send = pl.pallas_call(
        functools.partial(place_kernel, n_seq, heads),
        out_shape=(
            jax.ShapeDtypeStruct((2 * heads,), i32),
            jax.ShapeDtypeStruct((n_seq, *block), bf16),
        ),
        in_specs=[smem, hbm],
        out_specs=(smem, hbm),
        scratch_shapes=[
            pltpu.SMEM((2 * n_seq,), i32),
            pltpu.VMEM((tile_rows, features), bf16),
            pltpu.SemaphoreType.DMA,
            pltpu.SemaphoreType.DMA((n_seq,)),
        ],
        compiler_params=pltpu.CompilerParams(vmem_limit_bytes=most_vmem),
        name="place_heads",
    )(head_slot, v2)
    value_main = swap(value_send, seq_axes)

    gains = lax.all_gather(jnp.stack([gain_q, gain_k]), "fsdp", axis=1, tiled=True)
    kq_send, grad_send, extra_send = call(
        functools.partial(norm_kernel, n_seq, heads),
        "normalize",
        [((n_seq, 2, *block), bf16), ((n_seq, *block), bf16), ((extra, 4, *block), bf16)],
        [smem] + [vmem] * 5,
        7 * heads,
        hbm_in=(1, 2, 3, 4),
        hbm_out=(0, 1, 2),
    )(order, q2, k2, v2, g2, gains)
    table = jnp.concatenate([mask_lists, tile_counts[:, :, None]], axis=2)
    table_main = lax.dynamic_index_in_dim(table, order[own], 0, keepdims=False).reshape(-1)
    table_extra = lax.dynamic_index_in_dim(table, order[n_seq + z_index], 0, keepdims=False)
    table_extra = lax.dynamic_index_in_dim(
        table_extra.reshape(n_z, n_x, most + 1), x_index, 1, keepdims=False
    )
    table_extra = jnp.concatenate([table_extra.reshape(-1), x_index[None]])
    extra_own = swap(after(extra_send, (value_main, table_main, table_extra)), "z")

    def attention(parts, name, n_query, at, outs, n_operands, passes, hbm_in=(), hbm_out=()):
        group = 2
        tile_f32 = pltpu.VMEM((n_tiles, *block), f32)
        tile_bf16 = pltpu.VMEM((n_tiles, *block), bf16)
        scratch = {"scores": pltpu.VMEM((group, most, *block), f32)}
        if "forward" in parts:
            scratch |= {"vt": tile_bf16, "dv": tile_f32}
        if "backward" in parts:
            scratch |= {"kt": tile_bf16, "dk": tile_f32, "sums": pltpu.VMEM((2, 8, head_width), f32)}
            scratch["dprobs"] = scratch["scores"]
        if not at["ahead"]:
            scratch = {n: v for n, v in scratch.items() if n not in ("kt", "vt")}
            scratch["kv"] = pltpu.VMEM((n_tiles, 2, *block), bf16)
        at = {**at, "scratch": list(scratch), "results": list(outs)}
        return call(
            functools.partial(attention_kernel, parts, most, n_query, n_tiles, group, at),
            name,
            list(outs.values()),
            [smem] + [vmem] * n_operands,
            10 * n_tiles,
            flops=n_query * most * passes * 2 * tile_rows * tile_rows * head_width,
            scratch=list(scratch.values()),
            hbm_in=hbm_in,
            hbm_out=hbm_out,
        )

    rows_of = lambda n: ((n, tile_rows), f32)

    def shift(values, s):
        return lax.ppermute(values, "x", [(x, (x + s) % n_x) for x in range(n_x)])

    kv_own = extra_own[:, 2:4]
    kv_shifted = [shift(kv_own, s) for s in range(1, n_x)]
    grad_main = swap(after(grad_send, extra_own), seq_axes)
    kq_main = swap(after(kq_send, (grad_main, kv_shifted)), seq_axes)
    kv_shifted = after(kv_shifted, grad_main)
    odq_extra, lse_extra, gain_extra, *dkv_parts = attention(
        ("forward", "backward"),
        "attention_second",
        n_z,
        {
            "operands": ["own", *(f"kv{s}" for s in range(1, n_x))],
            "key": lambda r, t: r["kv"][t, 0],
            "value": lambda r, t: r["kv"][t, 1],
            "query": lambda r, i: r["own"][i, 0],
            "grad": lambda r, i: r["own"][i, 1],
            "ahead": False,
            "prologue": functools.partial(load_shifted, n_x, n_z),
            "epilogue": functools.partial(store_shifted, n_x, n_z),
            "store_out": setter("odq", lambda i: (i, 0)),
            "store_dq": setter("odq", lambda i: (i, 1)),
            "store_dk": store_part(0),
            "store_dv": store_part(1),
        },
        {
            "odq": ((n_z, 2, *block), bf16),
            "lse": rows_of(n_z),
            "gains": ((2, head_width), f32),
            **{f"part{s}": ((n_z, 2, *block), bf16) for s in range(n_x)},
        },
        n_x,
        20,
    )(table_extra, extra_own, *kv_shifted)
    relayed = shift(dkv_parts[2], n_x - 1)
    (joined,) = call(add_kernel, "add_parts", [((n_z, 2, *block), bf16)], [vmem] * 2, 6 * n_z)(
        dkv_parts[3], relayed
    )
    dkv_parts = [dkv_parts[0], shift(dkv_parts[1], 1), shift(joined, n_x - 1)]
    main_at = {
        "ahead": True,
        "epilogue": functools.partial(every_tile, n_tiles),
        "key": lambda r, t: r["kq"][t, 0],
        "value": lambda r, t: r["v"][t],
        "query": lambda r, i: r["kq"][i, 1],
        "grad": lambda r, i: r["g"][i],
    }
    (extra_back,) = call(
        collect_kernel, "collect", [((n_z, 4, *block), bf16)], [vmem] * 4, 12 * n_z
    )(odq_extra, *dkv_parts)
    extra_home = swap(after(extra_back, kq_main), "z")
    odv_main, lse_main, delta_main = attention(
        ("forward",),
        "forward_first",
        n_tiles,
        {
            **main_at,
            "operands": ["kq", "v", "g"],
            "store_out": setter("odv", lambda i: (i, 0)),
            "store_dv": setter("odv", lambda t: (t, 1)),
        },
        {"odv": ((n_tiles, 2, *block), bf16), "lse": rows_of(n_tiles), "delta": rows_of(n_tiles)},
        3,
        10,
        hbm_in=(1, 2, 3),
        hbm_out=(0,),
    )(table_main, kq_main, value_main, grad_main)
    odv_home = swap(after(odv_main, extra_home), seq_axes)
    dqk_main, gain_main = attention(
        ("backward",),
        "backward_first",
        n_tiles,
        {
            **main_at,
            "operands": ["kq", "v", "g", "lse", "delta"],
            "store_dq": setter("dqk", lambda i: (i, pl.ds(0, tile_rows))),
            "store_dk": store_dk_first,
        },
        {"dqk": ((n_tiles, 2 * tile_rows + shared_rows, head_width), bf16), "gains": ((2, head_width), f32)},
        5,
        16,
        hbm_in=(1, 2, 3),
        hbm_out=(0,),
    )(table_main, kq_main, value_main, grad_main, lse_main, delta_main)

    gain_sums = lax.psum(jnp.concatenate([gain_main, gain_extra]), "fsdp")
    dqk_shape = (n_tiles, 2 * tile_rows + shared_rows, head_width)
    dqk_main = pl.pallas_call(
        share_kernel,
        out_shape=jax.ShapeDtypeStruct(dqk_shape, bf16),
        in_specs=[vmem, vmem, hbm],
        out_specs=hbm,
        input_output_aliases={2: 0},
        scratch_shapes=[
            pltpu.VMEM((shared_rows, head_width), f32),
            pltpu.VMEM((shared_rows, head_width), bf16),
            pltpu.SemaphoreType.DMA((n_seq,)),
        ],
        compiler_params=pltpu.CompilerParams(vmem_limit_bytes=most_vmem),
        name="share_rows",
    )(gain_sums, lse_extra, dqk_main)
    dqk_home = swap(after(dqk_main, odv_home), seq_axes)

    wide = ((tile_rows, features), bf16)
    attn_out, grad_v = call(
        functools.partial(merge_kernel, n_seq, heads),
        "merge_heads",
        [wide, wide],
        [smem, vmem, vmem],
        4 * heads,
        hbm_in=(1, 2),
        hbm_out=(0, 1),
    )(order, odv_home, extra_home)
    grad_q, grad_k = call(
        functools.partial(back_kernel, n_seq, heads),
        "gradients_home",
        [wide, wide],
        [smem] + [vmem] * 5,
        6 * heads,
        hbm_in=(2, 1, 3, 4),
        hbm_out=(0, 1),
        lazy=True,
    )(order, dqk_home, extra_home, q2, k2, gains)

    per = heads // n_f
    lse_slots, share_q, share_k = call(
        functools.partial(finish_kernel, n_x, n_z, heads, per),
        "finish",
        [((2, n_tiles, tile_rows), f32), ((per, head_width), f32), ((per, head_width), f32)],
        [smem] * 3 + [vmem] * 3 + [hbm],
        32,
        scratch=[
            pltpu.VMEM((n_seq, shared_rows, head_width), bf16),
            pltpu.VMEM((n_seq, shared_rows, head_width), f32),
            pltpu.SemaphoreType.DMA,
        ],
        room=most_vmem,
    )(
        order,
        head_slot,
        jnp.stack([own, f_index]),
        lse_main,
        gain_q.reshape(per, head_width),
        gain_k.reshape(per, head_width),
        dqk_home,
    )
    whole = lambda a: a.reshape(1, tile_rows, features)
    return (
        whole(attn_out),
        lse_slots.reshape(1, 2, n_tiles * tile_rows),
        whole(grad_q),
        whole(grad_k),
        whole(grad_v),
        share_q.reshape(-1),
        share_k.reshape(-1),
    )


def solution(mesh):
    n_seq, n_f = mesh.devices.shape
    n_z = 8
    grid = Mesh(mesh.devices.reshape(n_z, n_seq // n_z, n_f), ("z", "x", "fsdp"))
    rows = P("fsdp", ("z", "x"), None)
    in_specs = (rows,) * 4 + (P("fsdp"),) * 2 + (P(),) * 3
    out_specs = (rows,) * 5 + (P("fsdp"),) * 2
    return jax.shard_map(shards, mesh=grid, in_specs=in_specs, out_specs=out_specs, check_vma=False)
```

```python
import functools
import math

import jax
import jax.numpy as jnp
from jax import lax
from jax.experimental import pallas as pl
from jax.experimental.pallas import tpu as pltpu
from jax.sharding import Mesh, PartitionSpec as P

norm_eps = 1e-06
head_width = 128
tile_rows = 128
block = (tile_rows, head_width)
log2e = 1.4426950408889634
ln2 = 0.6931471805599453
masked_out = -1e30
unrolled = 4
vmem_bytes = 26 * 2**20
most_vmem = 60 * 2**20

bf16 = jnp.bfloat16
f32 = jnp.float32
i32 = jnp.int32

vmem = pl.BlockSpec(memory_space=pltpu.VMEM)
smem = pl.BlockSpec(memory_space=pltpu.SMEM)
hbm = pl.BlockSpec(memory_space=pltpu.HBM)


def dot(a, b, contract):
    dims = ((contract[:1], contract[1:]), ((), ()))
    return lax.dot_general(a, b, dims, preferred_element_type=f32)


def staged(kernel, n_in, n_out, hbm_in, hbm_out, lazy, refs):
    ins, outs = list(refs[:n_in]), list(refs[n_in : n_in + n_out])
    rest = refs[n_in + n_out :]
    n_hbm = len(hbm_in) + len(hbm_out)
    scratch, buffers, sems = rest[: len(rest) - n_hbm - 1], rest[len(rest) - n_hbm - 1 : -1], rest[-1]
    reads, writes = {}, {}
    for c, i in enumerate(hbm_in):
        reads[i] = pltpu.make_async_copy(ins[i], buffers[c], sems.at[c])
        reads[i].start()
        ins[i] = buffers[c]
    for c, o in enumerate(hbm_out, len(hbm_in)):
        writes[o] = pltpu.make_async_copy(buffers[c], outs[o], sems.at[c])
        outs[o] = buffers[c]
    if lazy:
        kernel(*ins, *outs, *scratch, ready=lambda i: reads[i].wait(), flush=lambda o: writes[o].start())
    else:
        for i in hbm_in:
            reads[i].wait()
        kernel(*ins, *outs, *scratch)
        for o in hbm_out:
            writes[o].start()
    for o in hbm_out:
        writes[o].wait()


def call(kernel, name, outs, in_specs, tiles_moved, flops=0, scratch=(), smem_outs=(), hbm_in=(), hbm_out=(), lazy=False, room=vmem_bytes):
    def run(*operands):
        specs = [hbm if i in hbm_in else spec for i, spec in enumerate(in_specs)]
        kinds = (smem if n in smem_outs else hbm if n in hbm_out else vmem for n in range(len(outs)))
        buffers = [pltpu.VMEM(operands[i].shape, operands[i].dtype) for i in hbm_in]
        buffers += [pltpu.VMEM(*outs[o]) for o in hbm_out]
        body, extra = kernel, []
        if buffers:
            body = lambda *refs: staged(kernel, len(specs), len(outs), hbm_in, hbm_out, lazy, refs)
            extra = [*buffers, pltpu.SemaphoreType.DMA((len(buffers),))]
        return pl.pallas_call(
            body,
            out_shape=tuple(jax.ShapeDtypeStruct(*o) for o in outs),
            in_specs=specs,
            out_specs=tuple(kinds),
            scratch_shapes=[*scratch, *extra],
            compiler_params=pltpu.CompilerParams(
                vmem_limit_bytes=most_vmem if buffers else room
            ),
            cost_estimate=pl.CostEstimate(
                flops=flops, bytes_accessed=tiles_moved * tile_rows * head_width * 2, transcendentals=0
            ),
            name=name,
        )(*operands)

    return run


def cols(head):
    start = head * head_width
    if not isinstance(head, int):
        start = pl.multiple_of(start, head_width)
    return pl.ds(start, head_width)


def place_kernel(n_seq, heads, slot_ref, x_hbm, order_ref, main_hbm, held_ref, x_ref, read_sem, write_sems):
    read = pltpu.make_async_copy(x_hbm, x_ref, read_sem)
    read.start()

    @pl.loop(0, 2 * n_seq)
    def _(s):
        held_ref[s] = -1

    @pl.loop(0, heads)
    def _(h):
        held_ref[slot_ref[h]] = h

    def place(position, head):
        order_ref[position] = head
        order_ref[heads + head] = position

    def step(d, used):
        low, high = held_ref[2 * d], held_ref[2 * d + 1]
        place(d, jnp.where(low >= 0, low, high))
        both = jnp.logical_and(low >= 0, high >= 0)

        @pl.when(both)
        def _():
            place(used, high)

        return used + both.astype(i32)

    lax.fori_loop(0, n_seq, step, jnp.int32(n_seq))
    read.wait()
    writes = [
        pltpu.make_async_copy(x_ref.at[:, cols(order_ref[d])], main_hbm.at[d], write_sems.at[d])
        for d in range(n_seq)
    ]
    for write in writes:
        write.start()
    for write in writes:
        write.wait()


def norm_kernel(n_seq, heads, order_ref, q_ref, k_ref, v_ref, do_ref, gain_ref, kq_ref, grad_ref, extra_ref):
    for p in range(n_seq):
        grad_ref[p] = do_ref[:, cols(order_ref[p])]
    for which, x_ref in ((1, q_ref), (0, k_ref)):
        total = jnp.zeros(block, f32)
        for head in range(heads):
            x = x_ref[:, cols(head)].astype(f32)
            total += x * x
        mean = jnp.sum(total, axis=1, keepdims=True) * (1.0 / (heads * head_width))
        inverse = jnp.broadcast_to(lax.rsqrt(mean + norm_eps), block)
        for p in range(heads):
            at = cols(order_ref[p])
            gain = gain_ref[1 - which : 2 - which, at].astype(f32)
            normed = (x_ref[:, at].astype(f32) * inverse * gain).astype(bf16)
            if p < n_seq:
                kq_ref[p, which] = normed
            else:
                extra_ref[p - n_seq, 2 if which == 0 else 0] = normed
    for p in range(n_seq, heads):
        extra_ref[p - n_seq, 1] = do_ref[:, cols(order_ref[p])]
        extra_ref[p - n_seq, 3] = v_ref[:, cols(order_ref[p])]


def merge_kernel(n_seq, heads, order_ref, main_ref, extra_ref, out_ref, grad_v_ref):
    for p in range(heads):
        at = cols(order_ref[p])
        out_ref[:, at] = main_ref[p, 0] if p < n_seq else extra_ref[p - n_seq, 0]
        grad_v_ref[:, at] = main_ref[p, 1] if p < n_seq else extra_ref[p - n_seq, 3]


def back_kernel(n_seq, heads, order_ref, main_ref, extra_ref, q_ref, k_ref, gain_ref, gq_ref, gk_ref, ready, flush):
    ready(2)
    ready(1)
    scale = 1.0 / (heads * head_width)
    for which, x_ref, out_ref in ((0, q_ref, gq_ref), (1, k_ref, gk_ref)):
        ready(3 + which)

        def pieces(p):
            at = cols(order_ref[p])
            up = main_ref[p, pl.ds(which * tile_rows, tile_rows)] if p < n_seq else extra_ref[p - n_seq, 1 + which]
            gain = gain_ref[which : which + 1, at].astype(f32)
            return at, x_ref[:, at].astype(f32), gain * up.astype(f32)

        squares = jnp.zeros(block, f32)
        inner = jnp.zeros(block, f32)
        for p in range(heads):
            at, x, weighted = pieces(p)
            squares += x * x
            inner += weighted * x
        inverse = lax.rsqrt(jnp.sum(squares, axis=1, keepdims=True) * scale + norm_eps)
        pull = inverse * inverse * inverse * (jnp.sum(inner, axis=1, keepdims=True) * scale)
        inverse = jnp.broadcast_to(inverse, block)
        pull = jnp.broadcast_to(pull, block)
        for p in range(heads):
            at, x, weighted = pieces(p)
            out_ref[:, at] = (inverse * weighted - x * pull).astype(bf16)
        flush(which)


def fold_rows(values, combine):
    return combine(values.reshape(values.shape[0] // 8, 8, values.shape[1]), axis=0)


def attention_kernel(parts, most, n_query, n_tiles, group, at, *refs):
    names = ["table", *at["operands"], *at["results"], *at["scratch"]]
    r = dict(zip(names, refs))
    table = r["table"]
    stride = most + 1
    score_scale = log2e / math.sqrt(head_width)
    grad_scale = 1.0 / math.sqrt(head_width)
    key, value, query_of, grad_of = (
        functools.partial(at[k], r) for k in ("key", "value", "query", "grad")
    )
    forward, backward = "forward" in parts, "backward" in parts

    if "prologue" in at:
        at["prologue"](r)
    ahead = at["ahead"]

    @pl.loop(0, n_tiles // unrolled)
    def _(step):
        for t in [step * unrolled + u for u in range(unrolled)]:
            if forward:
                r["dv"][t] = jnp.zeros(block, f32)
            if backward:
                r["dk"][t] = jnp.zeros(block, f32)
            if forward and ahead:
                r["vt"][t] = value(t).T
            if backward and ahead:
                r["kt"][t] = key(t).T

    if backward:
        r["sums"][...] = jnp.zeros(r["sums"].shape, f32)

    def turned(name, t):
        if ahead:
            return r[name][t]
        return (value(t) if name == "vt" else key(t)).T

    def body(count, tiles, counts):
        for a, (i, n) in enumerate(zip(tiles, counts)):
            query, grad = query_of(i), grad_of(i)
            listed = [table[i * stride + j] for j in range(count)]

            def scores(j):
                s = dot(key(listed[j]), query, (1, 1)) * score_scale
                return jnp.where(j < n, s, masked_out) if j else s

            if forward:
                scratch = r["scores"]
                high = None
                for j in range(count):
                    s = scores(j)
                    scratch[a, j] = s
                    peak = fold_rows(s, jnp.max)
                    high = peak if high is None else jnp.maximum(high, peak)
                high = jnp.max(high, axis=0, keepdims=True)
                total = None
                for j in range(count):
                    p = jnp.exp2(scratch[a, j] - high)
                    scratch[a, j] = p
                    part = fold_rows(p, jnp.sum)
                    total = part if total is None else total + part
                total = jnp.sum(total, axis=0, keepdims=True)
                r["lse"][pl.ds(i, 1), :] = high * ln2 + jnp.log(total)
                inverse = 1.0 / total
                probs = [(scratch[a, j] * inverse).astype(bf16) for j in range(count)]
                values_t = jnp.concatenate([turned("vt", t) for t in listed], axis=1)
                out_t = dot(values_t, jnp.concatenate(probs, axis=0), (1, 0)).astype(bf16)
                at["store_out"](r, i, out_t.T)
                delta = jnp.sum(grad.T.astype(f32) * out_t.astype(f32), axis=0, keepdims=True)
                for j, t in enumerate(listed):
                    r["dv"][t] += dot(probs[j], grad, (1, 0))
                if not backward:
                    r["delta"][pl.ds(i, 1), :] = delta
            if backward:
                if not forward:
                    delta = r["delta"][pl.ds(i, 1), :]
                    lse = r["lse"][pl.ds(i, 1), :] * log2e
                if not forward:
                    for j in range(count):
                        r["scores"][a, j] = scores(j)
                for j, t in enumerate(listed):
                    r["dprobs"][a, j] = dot(value(t), grad, (1, 1))
                dscores = []
                for j in range(count):
                    s = r["scores"][a, j]
                    p = s * inverse if forward else jnp.exp2(s - lse)
                    dscores.append((p * (r["dprobs"][a, j] - delta)).astype(bf16))
                for j, t in enumerate(listed):
                    r["dk"][t] += dot(dscores[j], query, (1, 0))
                keys_t = jnp.concatenate([turned("kt", t) for t in listed], axis=1)
                dq_t = dot(keys_t, jnp.concatenate(dscores, axis=0), (1, 0)) * grad_scale
                dq = dq_t.astype(bf16).T
                at["store_dq"](r, i, dq)
                r["sums"][0] += fold_rows(dq.astype(f32) * query.astype(f32), jnp.sum)

    @pl.loop(0, n_query // group)
    def _(g):
        tiles = [g * group + a for a in range(group)]
        counts = [table[t * stride + most] for t in tiles]
        top = functools.reduce(jnp.maximum, counts)
        for static_count in range(1, most + 1):

            @pl.when(top == static_count)
            def _():
                body(static_count, tiles, counts)

    def store_grads(t, where):
        if forward:
            at["store_dv"](r, where, r["dv"][t].astype(bf16))
        if backward:
            dk = (r["dk"][t] * grad_scale).astype(bf16)
            at["store_dk"](r, where, dk)
            r["sums"][1] += fold_rows(dk.astype(f32) * key(t).astype(f32), jnp.sum)

    at["epilogue"](r, store_grads)

    if backward:
        for m in range(2):
            r["gains"][m : m + 1, :] = jnp.sum(r["sums"][m], axis=0, keepdims=True)


def setter(name, where):
    def store(r, i, values):
        r[name][where(i)] = values

    return store


def store_dk_first(r, t, values):
    r["dqk"][t, pl.ds(tile_rows, tile_rows)] = values
    r["dqk"][t, pl.ds(2 * tile_rows, shared_rows)] = jnp.zeros((shared_rows, head_width), bf16)


def every_tile(n_tiles, r, store):
    @pl.loop(0, n_tiles // unrolled)
    def _(step):
        for u in range(unrolled):
            store(step * unrolled + u, step * unrolled + u)


def load_shifted(n_x, n_z, r):
    x_index = r["table"][r["table"].shape[0] - 1]
    for s in range(n_x):
        x = lax.rem(x_index + n_x - s, n_x)
        for z in range(n_z):
            name, at = ("own" if s == 0 else f"kv{s}"), z
            if s == 2 and z >= n_z // 2:
                name, at = "kv2_rest", z - n_z // 2
            for m in range(2):
                r["kv"][z * n_x + x, m] = r[name][at, m + 2 if s == 0 else m]


def store_shifted(n_x, n_z, r, store):
    x_index = r["table"][r["table"].shape[0] - 1]
    for s in range(n_x):
        x = lax.rem(x_index + s, n_x)

        @pl.loop(0, n_z)
        def _(z):
            store(z * n_x + x, (s, z))


def store_part(m):
    def store(r, where, values):
        s, z = where
        r[f"part{s}"][z, m] = values

    return store


def add_kernel(one_ref, two_ref, sum_ref):
    @pl.loop(0, sum_ref.shape[0])
    def _(z):
        sum_ref[z] = (one_ref[z].astype(f32) + two_ref[z].astype(f32)).astype(bf16)


def collect_kernel(odq_ref, *refs):
    parts, back_ref = refs[:-1], refs[-1]

    @pl.loop(0, back_ref.shape[0])
    def _(z):
        for m in range(2):
            back_ref[z, m] = odq_ref[z, m]
            total = sum(part[z, m].astype(f32) for part in parts)
            back_ref[z, 2 + m] = total.astype(bf16)


shared_rows = 32


def share_kernel(sums_ref, lse_ref, unused_hbm, back_hbm, terms_ref, rows_ref, sems):
    value = sums_ref[...]
    for term in range(2):
        part = value.astype(bf16).astype(f32)
        terms_ref[4 * term : 4 * term + 4, :] = part
        value = value - part
    value = lse_ref[...]
    for term in range(1, 4):
        part = value.astype(bf16).astype(f32)
        terms_ref[8 * term : 8 * term + 8, :] = part
        value = value - part
    rows_ref[...] = terms_ref[...].astype(bf16)
    n_seq, n_rows = back_hbm.shape[:2]
    last = pl.ds(n_rows - shared_rows, shared_rows)
    copies = [pltpu.make_async_copy(rows_ref, back_hbm.at[d, last], sems.at[d]) for d in range(n_seq)]
    for copy in copies:
        copy.start()
    for copy in copies:
        copy.wait()


def finish_kernel(n_x, n_z, heads, per, order_ref, slot_ref, here_ref, lse_ref, gq_ref, gk_ref, home_hbm, out_ref, sq_ref, sk_ref, rows_ref, shared_ref, held_ref, sem):
    n_seq = n_x * n_z
    own, f_index = here_ref[0], here_ref[1]
    last = pl.ds(home_hbm.shape[1] - shared_rows, shared_rows)
    copy = pltpu.make_async_copy(home_hbm.at[:, last], rows_ref, sem)
    copy.start()
    copy.wait()
    shared_ref[...] = rows_ref[...].astype(f32)

    def row(device, line):
        lines = [8 * t + line for t in range(1, 4)] if line < n_z else [line - n_z, line - n_z + 4]
        return sum(shared_ref[device, n : n + 1, :] for n in lines)

    held_ref[...] = jnp.zeros(held_ref.shape, f32)
    held_ref[lax.rem(slot_ref[order_ref[own]], 2)] = lse_ref[...]

    @pl.loop(0, heads - n_seq)
    def _(e):
        slot = slot_ref[order_ref[n_seq + e]]

        @pl.when(lax.div(slot, 2) == own)
        def _():
            for x in range(n_x):
                for z in range(n_z):
                    at = z * n_x + x
                    held_ref[lax.rem(slot, 2), at : at + 1, :] = row(e * n_x + x, z)

    for s in range(2):
        for t in range(n_seq):
            out_ref[s : s + 1, cols(t)] = held_ref[s, t : t + 1, :]

    factor = 1.0 / math.sqrt(n_seq * tile_rows * (heads // per))
    for j in range(per):
        position = order_ref[heads + f_index * per + j]
        for m, (gain_ref, out) in enumerate(((gq_ref, sq_ref), (gk_ref, sk_ref))):
            first = row(jnp.minimum(position, n_seq - 1), n_z + m)
            spread = jnp.maximum(position - n_seq, 0) * n_x
            second = sum(row(spread + x, n_z + 2 + m) for x in range(n_x))
            total = jnp.where(position < n_seq, first, second)
            out[j : j + 1, :] = total / gain_ref[j : j + 1, :].astype(f32) * factor


def after(values, done):
    return lax.optimization_barrier((values, done))[0]


def shards(query_in, key_in, value_in, out_grad, gain_q, gain_k, mask_lists, tile_counts, head_slot):
    n_x, n_z, n_f = lax.axis_size("x"), lax.axis_size("z"), lax.axis_size("fsdp")
    n_seq = n_x * n_z
    x_index, z_index, f_index = lax.axis_index("x"), lax.axis_index("z"), lax.axis_index("fsdp")
    own = z_index * n_x + x_index
    heads, n_tiles, most = mask_lists.shape
    extra = heads - n_seq
    features = heads * head_width
    seq_axes = ("z", "x")
    q2, k2, v2, g2 = (a.reshape(tile_rows, features) for a in (query_in, key_in, value_in, out_grad))

    def swap(values, axes):
        return lax.all_to_all(values, axes, split_axis=0, concat_axis=0, tiled=True)

    order, value_send = pl.pallas_call(
        functools.partial(place_kernel, n_seq, heads),
        out_shape=(
            jax.ShapeDtypeStruct((2 * heads,), i32),
            jax.ShapeDtypeStruct((n_seq, *block), bf16),
        ),
        in_specs=[smem, hbm],
        out_specs=(smem, hbm),
        scratch_shapes=[
            pltpu.SMEM((2 * n_seq,), i32),
            pltpu.VMEM((tile_rows, features), bf16),
            pltpu.SemaphoreType.DMA,
            pltpu.SemaphoreType.DMA((n_seq,)),
        ],
        compiler_params=pltpu.CompilerParams(vmem_limit_bytes=most_vmem),
        name="place_heads",
    )(head_slot, v2)
    value_main = swap(value_send, seq_axes)

    gains = lax.all_gather(jnp.stack([gain_q, gain_k]), "fsdp", axis=1, tiled=True)
    kq_send, grad_send, extra_send = call(
        functools.partial(norm_kernel, n_seq, heads),
        "normalize",
        [((n_seq, 2, *block), bf16), ((n_seq, *block), bf16), ((extra, 4, *block), bf16)],
        [smem] + [vmem] * 5,
        7 * heads,
        hbm_in=(1, 2, 3, 4),
        hbm_out=(0, 1, 2),
    )(order, q2, k2, v2, g2, gains)
    table = jnp.concatenate([mask_lists, tile_counts[:, :, None]], axis=2)
    table_main = lax.dynamic_index_in_dim(table, order[own], 0, keepdims=False).reshape(-1)
    table_extra = lax.dynamic_index_in_dim(table, order[n_seq + z_index], 0, keepdims=False)
    table_extra = lax.dynamic_index_in_dim(
        table_extra.reshape(n_z, n_x, most + 1), x_index, 1, keepdims=False
    )
    table_extra = jnp.concatenate([table_extra.reshape(-1), x_index[None]])
    extra_own = swap(after(extra_send, (value_main, table_main, table_extra)), "z")

    def attention(parts, name, n_query, at, outs, n_operands, passes, hbm_in=(), hbm_out=()):
        group = 2
        tile_f32 = pltpu.VMEM((n_tiles, *block), f32)
        tile_bf16 = pltpu.VMEM((n_tiles, *block), bf16)
        scratch = {"scores": pltpu.VMEM((group, most, *block), f32)}
        if "forward" in parts:
            scratch |= {"vt": tile_bf16, "dv": tile_f32}
        if "backward" in parts:
            scratch |= {"kt": tile_bf16, "dk": tile_f32, "sums": pltpu.VMEM((2, 8, head_width), f32)}
            scratch["dprobs"] = scratch["scores"]
        if not at["ahead"]:
            scratch = {n: v for n, v in scratch.items() if n not in ("kt", "vt")}
            scratch["kv"] = pltpu.VMEM((n_tiles, 2, *block), bf16)
        at = {**at, "scratch": list(scratch), "results": list(outs)}
        return call(
            functools.partial(attention_kernel, parts, most, n_query, n_tiles, group, at),
            name,
            list(outs.values()),
            [smem] + [vmem] * n_operands,
            10 * n_tiles,
            flops=n_query * most * passes * 2 * tile_rows * tile_rows * head_width,
            scratch=list(scratch.values()),
            hbm_in=hbm_in,
            hbm_out=hbm_out,
        )

    rows_of = lambda n: ((n, tile_rows), f32)

    def shift(values, s):
        return lax.ppermute(values, "x", [(x, (x + s) % n_x) for x in range(n_x)])

    kv_own = extra_own[:, 2:4]
    kv_left, kv_right = shift(kv_own, 1), shift(kv_own, n_x - 1)
    half = n_z // 2
    kv_shifted = [kv_left, shift(kv_left[:half], 1), shift(kv_right[half:], n_x - 1), kv_right]
    grad_main = swap(after(grad_send, extra_own), seq_axes)
    kq_main = swap(after(kq_send, (grad_main, kv_shifted)), seq_axes)
    kv_shifted = after(kv_shifted, grad_main)
    odq_extra, lse_extra, gain_extra, *dkv_parts = attention(
        ("forward", "backward"),
        "attention_second",
        n_z,
        {
            "operands": ["own", "kv1", "kv2", "kv2_rest", "kv3"],
            "key": lambda r, t: r["kv"][t, 0],
            "value": lambda r, t: r["kv"][t, 1],
            "query": lambda r, i: r["own"][i, 0],
            "grad": lambda r, i: r["own"][i, 1],
            "ahead": False,
            "prologue": functools.partial(load_shifted, n_x, n_z),
            "epilogue": functools.partial(store_shifted, n_x, n_z),
            "store_out": setter("odq", lambda i: (i, 0)),
            "store_dq": setter("odq", lambda i: (i, 1)),
            "store_dk": store_part(0),
            "store_dv": store_part(1),
        },
        {
            "odq": ((n_z, 2, *block), bf16),
            "lse": rows_of(n_z),
            "gains": ((2, head_width), f32),
            **{f"part{s}": ((n_z, 2, *block), bf16) for s in range(n_x)},
        },
        n_x + 1,
        20,
    )(table_extra, extra_own, *kv_shifted)
    relayed = shift(dkv_parts[2], n_x - 1)
    (joined,) = call(add_kernel, "add_parts", [((n_z, 2, *block), bf16)], [vmem] * 2, 6 * n_z)(
        dkv_parts[3], relayed
    )
    dkv_parts = [dkv_parts[0], shift(dkv_parts[1], 1), shift(joined, n_x - 1)]
    main_at = {
        "ahead": True,
        "epilogue": functools.partial(every_tile, n_tiles),
        "key": lambda r, t: r["kq"][t, 0],
        "value": lambda r, t: r["v"][t],
        "query": lambda r, i: r["kq"][i, 1],
        "grad": lambda r, i: r["g"][i],
    }
    (extra_back,) = call(
        collect_kernel, "collect", [((n_z, 4, *block), bf16)], [vmem] * 4, 12 * n_z
    )(odq_extra, *dkv_parts)
    extra_home = swap(after(extra_back, kq_main), "z")
    odv_main, lse_main, delta_main = attention(
        ("forward",),
        "forward_first",
        n_tiles,
        {
            **main_at,
            "operands": ["kq", "v", "g"],
            "store_out": setter("odv", lambda i: (i, 0)),
            "store_dv": setter("odv", lambda t: (t, 1)),
        },
        {"odv": ((n_tiles, 2, *block), bf16), "lse": rows_of(n_tiles), "delta": rows_of(n_tiles)},
        3,
        10,
        hbm_in=(1, 2, 3),
        hbm_out=(0,),
    )(table_main, kq_main, value_main, grad_main)
    odv_home = swap(after(odv_main, extra_home), seq_axes)
    dqk_main, gain_main = attention(
        ("backward",),
        "backward_first",
        n_tiles,
        {
            **main_at,
            "operands": ["kq", "v", "g", "lse", "delta"],
            "store_dq": setter("dqk", lambda i: (i, pl.ds(0, tile_rows))),
            "store_dk": store_dk_first,
        },
        {"dqk": ((n_tiles, 2 * tile_rows + shared_rows, head_width), bf16), "gains": ((2, head_width), f32)},
        5,
        16,
        hbm_in=(1, 2, 3),
        hbm_out=(0,),
    )(table_main, kq_main, value_main, grad_main, lse_main, delta_main)

    gain_sums = lax.psum(jnp.concatenate([gain_main, gain_extra]), "fsdp")
    dqk_shape = (n_tiles, 2 * tile_rows + shared_rows, head_width)
    dqk_main = pl.pallas_call(
        share_kernel,
        out_shape=jax.ShapeDtypeStruct(dqk_shape, bf16),
        in_specs=[vmem, vmem, hbm],
        out_specs=hbm,
        input_output_aliases={2: 0},
        scratch_shapes=[
            pltpu.VMEM((shared_rows, head_width), f32),
            pltpu.VMEM((shared_rows, head_width), bf16),
            pltpu.SemaphoreType.DMA((n_seq,)),
        ],
        compiler_params=pltpu.CompilerParams(vmem_limit_bytes=most_vmem),
        name="share_rows",
    )(gain_sums, lse_extra, dqk_main)
    dqk_home = swap(after(dqk_main, odv_home), seq_axes)

    wide = ((tile_rows, features), bf16)
    attn_out, grad_v = call(
        functools.partial(merge_kernel, n_seq, heads),
        "merge_heads",
        [wide, wide],
        [smem, vmem, vmem],
        4 * heads,
        hbm_in=(1, 2),
        hbm_out=(0, 1),
    )(order, odv_home, extra_home)
    grad_q, grad_k = call(
        functools.partial(back_kernel, n_seq, heads),
        "gradients_home",
        [wide, wide],
        [smem] + [vmem] * 5,
        6 * heads,
        hbm_in=(2, 1, 3, 4),
        hbm_out=(0, 1),
        lazy=True,
    )(order, dqk_home, extra_home, q2, k2, gains)

    per = heads // n_f
    lse_slots, share_q, share_k = call(
        functools.partial(finish_kernel, n_x, n_z, heads, per),
        "finish",
        [((2, n_tiles * tile_rows), f32), ((per, head_width), f32), ((per, head_width), f32)],
        [smem] * 3 + [vmem] * 3 + [hbm],
        32,
        scratch=[
            pltpu.VMEM((n_seq, shared_rows, head_width), bf16),
            pltpu.VMEM((n_seq, shared_rows, head_width), f32),
            pltpu.VMEM((2, n_tiles, tile_rows), f32),
            pltpu.SemaphoreType.DMA,
        ],
        room=most_vmem,
    )(
        order,
        head_slot,
        jnp.stack([own, f_index]),
        lse_main,
        gain_q.reshape(per, head_width),
        gain_k.reshape(per, head_width),
        dqk_home,
    )
    whole = lambda a: a.reshape(1, tile_rows, features)
    return (
        whole(attn_out),
        lse_slots[None],
        whole(grad_q),
        whole(grad_k),
        whole(grad_v),
        share_q.reshape(-1),
        share_k.reshape(-1),
    )


def solution(mesh):
    n_seq, n_f = mesh.devices.shape
    n_z = 8
    grid = Mesh(mesh.devices.reshape(n_z, n_seq // n_z, n_f), ("z", "x", "fsdp"))
    rows = P("fsdp", ("z", "x"), None)
    in_specs = (rows,) * 4 + (P("fsdp"),) * 2 + (P(),) * 3
    out_specs = (rows,) * 5 + (P("fsdp"),) * 2
    return jax.shard_map(shards, mesh=grid, in_specs=in_specs, out_specs=out_specs, check_vma=False)
```

```python
import functools
import math

import jax
import jax.numpy as jnp
from jax import lax
from jax.experimental import pallas as pl
from jax.experimental.pallas import tpu as pltpu
from jax.sharding import Mesh, PartitionSpec as P

norm_eps = 1e-06
head_width = 128
tile_rows = 128
block = (tile_rows, head_width)
log2e = 1.4426950408889634
ln2 = 0.6931471805599453
masked_out = -1e30
unrolled = 4
vmem_bytes = 26 * 2**20
most_vmem = 60 * 2**20

bf16 = jnp.bfloat16
f32 = jnp.float32
i32 = jnp.int32

vmem = pl.BlockSpec(memory_space=pltpu.VMEM)
smem = pl.BlockSpec(memory_space=pltpu.SMEM)
hbm = pl.BlockSpec(memory_space=pltpu.HBM)


def dot(a, b, contract):
    dims = ((contract[:1], contract[1:]), ((), ()))
    return lax.dot_general(a, b, dims, preferred_element_type=f32)


def staged(kernel, n_in, n_out, hbm_in, hbm_out, lazy, refs):
    ins, outs = list(refs[:n_in]), list(refs[n_in : n_in + n_out])
    rest = refs[n_in + n_out :]
    n_hbm = len(hbm_in) + len(hbm_out)
    scratch, buffers, sems = rest[: len(rest) - n_hbm - 1], rest[len(rest) - n_hbm - 1 : -1], rest[-1]
    reads, writes = {}, {}
    for c, i in enumerate(hbm_in):
        reads[i] = pltpu.make_async_copy(ins[i], buffers[c], sems.at[c])
        reads[i].start()
        ins[i] = buffers[c]
    for c, o in enumerate(hbm_out, len(hbm_in)):
        writes[o] = pltpu.make_async_copy(buffers[c], outs[o], sems.at[c])
        outs[o] = buffers[c]
    if lazy:
        kernel(*ins, *outs, *scratch, ready=lambda i: reads[i].wait(), flush=lambda o: writes[o].start())
    else:
        for i in hbm_in:
            reads[i].wait()
        kernel(*ins, *outs, *scratch)
        for o in hbm_out:
            writes[o].start()
    for o in hbm_out:
        writes[o].wait()


def call(kernel, name, outs, in_specs, tiles_moved, flops=0, scratch=(), smem_outs=(), hbm_in=(), hbm_out=(), lazy=False):
    def run(*operands):
        specs = [hbm if i in hbm_in else spec for i, spec in enumerate(in_specs)]
        kinds = (smem if n in smem_outs else hbm if n in hbm_out else vmem for n in range(len(outs)))
        buffers = [pltpu.VMEM(operands[i].shape, operands[i].dtype) for i in hbm_in]
        buffers += [pltpu.VMEM(*outs[o]) for o in hbm_out]
        body, extra = kernel, []
        if buffers:
            body = lambda *refs: staged(kernel, len(specs), len(outs), hbm_in, hbm_out, lazy, refs)
            extra = [*buffers, pltpu.SemaphoreType.DMA((len(buffers),))]
        return pl.pallas_call(
            body,
            out_shape=tuple(jax.ShapeDtypeStruct(*o) for o in outs),
            in_specs=specs,
            out_specs=tuple(kinds),
            scratch_shapes=[*scratch, *extra],
            compiler_params=pltpu.CompilerParams(
                vmem_limit_bytes=most_vmem if buffers else vmem_bytes
            ),
            cost_estimate=pl.CostEstimate(
                flops=flops, bytes_accessed=tiles_moved * tile_rows * head_width * 2, transcendentals=0
            ),
            name=name,
        )(*operands)

    return run


def cols(head):
    start = head * head_width
    if not isinstance(head, int):
        start = pl.multiple_of(start, head_width)
    return pl.ds(start, head_width)


def place_kernel(n_seq, heads, slot_ref, x_hbm, order_ref, main_hbm, held_ref, x_ref, read_sem, write_sems):
    read = pltpu.make_async_copy(x_hbm, x_ref, read_sem)
    read.start()

    @pl.loop(0, 2 * n_seq)
    def _(s):
        held_ref[s] = -1

    @pl.loop(0, heads)
    def _(h):
        held_ref[slot_ref[h]] = h

    def place(position, head):
        order_ref[position] = head
        order_ref[heads + head] = position

    def step(d, used):
        low, high = held_ref[2 * d], held_ref[2 * d + 1]
        place(d, jnp.where(low >= 0, low, high))
        both = jnp.logical_and(low >= 0, high >= 0)

        @pl.when(both)
        def _():
            place(used, high)

        return used + both.astype(i32)

    lax.fori_loop(0, n_seq, step, jnp.int32(n_seq))
    read.wait()
    writes = [
        pltpu.make_async_copy(x_ref.at[:, cols(order_ref[d])], main_hbm.at[d], write_sems.at[d])
        for d in range(n_seq)
    ]
    for write in writes:
        write.start()
    for write in writes:
        write.wait()


def norm_kernel(n_seq, heads, order_ref, q_ref, k_ref, v_ref, do_ref, gain_ref, kq_ref, grad_ref, extra_ref):
    for p in range(n_seq):
        grad_ref[p] = do_ref[:, cols(order_ref[p])]
    for which, x_ref in ((1, q_ref), (0, k_ref)):
        total = jnp.zeros(block, f32)
        for head in range(heads):
            x = x_ref[:, cols(head)].astype(f32)
            total += x * x
        mean = jnp.sum(total, axis=1, keepdims=True) * (1.0 / (heads * head_width))
        inverse = jnp.broadcast_to(lax.rsqrt(mean + norm_eps), block)
        for p in range(heads):
            at = cols(order_ref[p])
            gain = gain_ref[1 - which : 2 - which, at].astype(f32)
            normed = (x_ref[:, at].astype(f32) * inverse * gain).astype(bf16)
            if p < n_seq:
                kq_ref[p, which] = normed
            else:
                extra_ref[p - n_seq, 2 if which == 0 else 0] = normed
    for p in range(n_seq, heads):
        extra_ref[p - n_seq, 1] = do_ref[:, cols(order_ref[p])]
        extra_ref[p - n_seq, 3] = v_ref[:, cols(order_ref[p])]


def merge_kernel(n_seq, heads, order_ref, main_ref, extra_ref, out_ref, grad_v_ref):
    for p in range(heads):
        at = cols(order_ref[p])
        out_ref[:, at] = main_ref[p, 0] if p < n_seq else extra_ref[p - n_seq, 0]
        grad_v_ref[:, at] = main_ref[p, 1] if p < n_seq else extra_ref[p - n_seq, 3]


def back_kernel(n_x, n_z, heads, per, order_ref, main_ref, extra_ref, q_ref, k_ref, gain_ref, *refs, ready, flush):
    n_seq = n_x * n_z
    finish_in, (gq_ref, gk_ref), finish_out = refs[:5], refs[5:7], refs[7:]
    ready(2)
    ready(1)
    scale = 1.0 / (heads * head_width)
    for which, x_ref, out_ref in ((0, q_ref, gq_ref), (1, k_ref, gk_ref)):
        ready(3 + which)

        def pieces(p):
            at = cols(order_ref[p])
            up = main_ref[p, pl.ds(which * tile_rows, tile_rows)] if p < n_seq else extra_ref[p - n_seq, 1 + which]
            gain = gain_ref[which : which + 1, at].astype(f32)
            return at, x_ref[:, at].astype(f32), gain * up.astype(f32)

        squares = jnp.zeros(block, f32)
        inner = jnp.zeros(block, f32)
        for p in range(heads):
            at, x, weighted = pieces(p)
            squares += x * x
            inner += weighted * x
        inverse = lax.rsqrt(jnp.sum(squares, axis=1, keepdims=True) * scale + norm_eps)
        pull = inverse * inverse * inverse * (jnp.sum(inner, axis=1, keepdims=True) * scale)
        inverse = jnp.broadcast_to(inverse, block)
        pull = jnp.broadcast_to(pull, block)
        for p in range(heads):
            at, x, weighted = pieces(p)
            out_ref[:, at] = (inverse * weighted - x * pull).astype(bf16)
        flush(which)
    finish(n_x, n_z, heads, per, order_ref, main_ref, *finish_in, *finish_out)


def fold_rows(values, combine):
    return combine(values.reshape(values.shape[0] // 8, 8, values.shape[1]), axis=0)


def attention_kernel(parts, most, n_query, n_tiles, group, at, *refs):
    names = ["table", *at["operands"], *at["results"], *at["scratch"]]
    r = dict(zip(names, refs))
    table = r["table"]
    stride = most + 1
    score_scale = log2e / math.sqrt(head_width)
    grad_scale = 1.0 / math.sqrt(head_width)
    key, value, query_of, grad_of = (
        functools.partial(at[k], r) for k in ("key", "value", "query", "grad")
    )
    forward, backward = "forward" in parts, "backward" in parts

    if "prologue" in at:
        at["prologue"](r)
    ahead = at["ahead"]

    @pl.loop(0, n_tiles // unrolled)
    def _(step):
        for t in [step * unrolled + u for u in range(unrolled)]:
            if forward:
                r["dv"][t] = jnp.zeros(block, f32)
            if backward:
                r["dk"][t] = jnp.zeros(block, f32)
            if forward and ahead:
                r["vt"][t] = value(t).T
            if backward and ahead:
                r["kt"][t] = key(t).T

    if backward:
        r["sums"][...] = jnp.zeros(r["sums"].shape, f32)

    def turned(name, t):
        if ahead:
            return r[name][t]
        return (value(t) if name == "vt" else key(t)).T

    def body(count, tiles, counts):
        for a, (i, n) in enumerate(zip(tiles, counts)):
            query, grad = query_of(i), grad_of(i)
            listed = [table[i * stride + j] for j in range(count)]

            def scores(j):
                s = dot(key(listed[j]), query, (1, 1)) * score_scale
                return jnp.where(j < n, s, masked_out) if j else s

            if forward:
                scratch = r["scores"]
                high = None
                for j in range(count):
                    s = scores(j)
                    scratch[a, j] = s
                    peak = fold_rows(s, jnp.max)
                    high = peak if high is None else jnp.maximum(high, peak)
                high = jnp.max(high, axis=0, keepdims=True)
                total = None
                for j in range(count):
                    p = jnp.exp2(scratch[a, j] - high)
                    scratch[a, j] = p
                    part = fold_rows(p, jnp.sum)
                    total = part if total is None else total + part
                total = jnp.sum(total, axis=0, keepdims=True)
                r["lse"][pl.ds(i, 1), :] = high * ln2 + jnp.log(total)
                inverse = 1.0 / total
                probs = [(scratch[a, j] * inverse).astype(bf16) for j in range(count)]
                values_t = jnp.concatenate([turned("vt", t) for t in listed], axis=1)
                out_t = dot(values_t, jnp.concatenate(probs, axis=0), (1, 0)).astype(bf16)
                at["store_out"](r, i, out_t.T)
                delta = jnp.sum(grad.T.astype(f32) * out_t.astype(f32), axis=0, keepdims=True)
                for j, t in enumerate(listed):
                    r["dv"][t] += dot(probs[j], grad, (1, 0))
                if not backward:
                    r["delta"][pl.ds(i, 1), :] = delta
            if backward:
                if not forward:
                    delta = r["delta"][pl.ds(i, 1), :]
                    lse = r["lse"][pl.ds(i, 1), :] * log2e
                if not forward:
                    for j in range(count):
                        r["scores"][a, j] = scores(j)
                for j, t in enumerate(listed):
                    r["dprobs"][a, j] = dot(value(t), grad, (1, 1))
                dscores = []
                for j in range(count):
                    s = r["scores"][a, j]
                    p = s * inverse if forward else jnp.exp2(s - lse)
                    dscores.append((p * (r["dprobs"][a, j] - delta)).astype(bf16))
                for j, t in enumerate(listed):
                    r["dk"][t] += dot(dscores[j], query, (1, 0))
                keys_t = jnp.concatenate([turned("kt", t) for t in listed], axis=1)
                dq_t = dot(keys_t, jnp.concatenate(dscores, axis=0), (1, 0)) * grad_scale
                dq = dq_t.astype(bf16).T
                at["store_dq"](r, i, dq)
                r["sums"][0] += fold_rows(dq.astype(f32) * query.astype(f32), jnp.sum)

    @pl.loop(0, n_query // group)
    def _(g):
        tiles = [g * group + a for a in range(group)]
        counts = [table[t * stride + most] for t in tiles]
        top = functools.reduce(jnp.maximum, counts)
        for static_count in range(1, most + 1):

            @pl.when(top == static_count)
            def _():
                body(static_count, tiles, counts)

    def store_grads(t, where):
        if forward:
            at["store_dv"](r, where, r["dv"][t].astype(bf16))
        if backward:
            dk = (r["dk"][t] * grad_scale).astype(bf16)
            at["store_dk"](r, where, dk)
            r["sums"][1] += fold_rows(dk.astype(f32) * key(t).astype(f32), jnp.sum)

    at["epilogue"](r, store_grads)

    if backward:
        for m in range(2):
            r["gains"][m : m + 1, :] = jnp.sum(r["sums"][m], axis=0, keepdims=True)


def setter(name, where):
    def store(r, i, values):
        r[name][where(i)] = values

    return store


def store_dk_first(r, t, values):
    r["dqk"][t, pl.ds(tile_rows, tile_rows)] = values
    r["dqk"][t, pl.ds(2 * tile_rows, shared_rows)] = jnp.zeros((shared_rows, head_width), bf16)


def every_tile(n_tiles, r, store):
    @pl.loop(0, n_tiles // unrolled)
    def _(step):
        for u in range(unrolled):
            store(step * unrolled + u, step * unrolled + u)


def load_shifted(n_x, n_z, r):
    x_index = r["table"][r["table"].shape[0] - 1]
    for s in range(n_x):
        x = lax.rem(x_index + n_x - s, n_x)
        for z in range(n_z):
            name, at = ("own" if s == 0 else f"kv{s}"), z
            if s == 2 and z >= n_z // 2:
                name, at = "kv2_rest", z - n_z // 2
            for m in range(2):
                r["kv"][z * n_x + x, m] = r[name][at, m + 2 if s == 0 else m]


def store_shifted(n_x, n_z, r, store):
    x_index = r["table"][r["table"].shape[0] - 1]
    for s in range(n_x):
        x = lax.rem(x_index + s, n_x)

        @pl.loop(0, n_z)
        def _(z):
            store(z * n_x + x, (s, z))


def store_part(m):
    def store(r, where, values):
        s, z = where
        r[f"part{s}"][z, m] = values

    return store


def add_kernel(one_ref, two_ref, sum_ref):
    @pl.loop(0, sum_ref.shape[0])
    def _(z):
        sum_ref[z] = (one_ref[z].astype(f32) + two_ref[z].astype(f32)).astype(bf16)


def collect_kernel(odq_ref, *refs):
    parts, back_ref = refs[:-1], refs[-1]

    @pl.loop(0, back_ref.shape[0])
    def _(z):
        for m in range(2):
            back_ref[z, m] = odq_ref[z, m]
            total = sum(part[z, m].astype(f32) for part in parts)
            back_ref[z, 2 + m] = total.astype(bf16)


shared_rows = 32


def share_kernel(sums_ref, lse_ref, unused_hbm, back_hbm, terms_ref, rows_ref, sems):
    value = sums_ref[...]
    for term in range(2):
        part = value.astype(bf16).astype(f32)
        terms_ref[4 * term : 4 * term + 4, :] = part
        value = value - part
    value = lse_ref[...]
    for term in range(1, 4):
        part = value.astype(bf16).astype(f32)
        terms_ref[8 * term : 8 * term + 8, :] = part
        value = value - part
    rows_ref[...] = terms_ref[...].astype(bf16)
    n_seq, n_rows = back_hbm.shape[:2]
    last = pl.ds(n_rows - shared_rows, shared_rows)
    copies = [pltpu.make_async_copy(rows_ref, back_hbm.at[d, last], sems.at[d]) for d in range(n_seq)]
    for copy in copies:
        copy.start()
    for copy in copies:
        copy.wait()


def finish(n_x, n_z, heads, per, order_ref, home_ref, slot_ref, here_ref, lse_ref, gq_ref, gk_ref, out_ref, sq_ref, sk_ref, shared_ref, held_ref):
    n_seq = n_x * n_z
    own, f_index = here_ref[0], here_ref[1]
    last = pl.ds(home_ref.shape[1] - shared_rows, shared_rows)
    for d in range(n_seq):
        shared_ref[d] = home_ref[d, last].astype(f32)

    def row(device, line):
        lines = [8 * t + line for t in range(1, 4)] if line < n_z else [line - n_z, line - n_z + 4]
        return sum(shared_ref[device, n : n + 1, :] for n in lines)

    held_ref[...] = jnp.zeros(held_ref.shape, f32)
    held_ref[lax.rem(slot_ref[order_ref[own]], 2)] = lse_ref[...]

    @pl.loop(0, heads - n_seq)
    def _(e):
        slot = slot_ref[order_ref[n_seq + e]]

        @pl.when(lax.div(slot, 2) == own)
        def _():
            for x in range(n_x):
                for z in range(n_z):
                    at = z * n_x + x
                    held_ref[lax.rem(slot, 2), at : at + 1, :] = row(e * n_x + x, z)

    for s in range(2):
        for t in range(n_seq):
            out_ref[s : s + 1, cols(t)] = held_ref[s, t : t + 1, :]

    factor = 1.0 / math.sqrt(n_seq * tile_rows * (heads // per))
    for j in range(per):
        position = order_ref[heads + f_index * per + j]
        for m, (gain_ref, out) in enumerate(((gq_ref, sq_ref), (gk_ref, sk_ref))):
            first = row(jnp.minimum(position, n_seq - 1), n_z + m)
            spread = jnp.maximum(position - n_seq, 0) * n_x
            second = sum(row(spread + x, n_z + 2 + m) for x in range(n_x))
            total = jnp.where(position < n_seq, first, second)
            out[j : j + 1, :] = total / gain_ref[j : j + 1, :].astype(f32) * factor


def after(values, done):
    return lax.optimization_barrier((values, done))[0]


def shards(query_in, key_in, value_in, out_grad, gain_q, gain_k, mask_lists, tile_counts, head_slot):
    n_x, n_z, n_f = lax.axis_size("x"), lax.axis_size("z"), lax.axis_size("fsdp")
    n_seq = n_x * n_z
    x_index, z_index, f_index = lax.axis_index("x"), lax.axis_index("z"), lax.axis_index("fsdp")
    own = z_index * n_x + x_index
    heads, n_tiles, most = mask_lists.shape
    extra = heads - n_seq
    features = heads * head_width
    seq_axes = ("z", "x")
    q2, k2, v2, g2 = (a.reshape(tile_rows, features) for a in (query_in, key_in, value_in, out_grad))

    def swap(values, axes):
        return lax.all_to_all(values, axes, split_axis=0, concat_axis=0, tiled=True)

    order, value_send = pl.pallas_call(
        functools.partial(place_kernel, n_seq, heads),
        out_shape=(
            jax.ShapeDtypeStruct((2 * heads,), i32),
            jax.ShapeDtypeStruct((n_seq, *block), bf16),
        ),
        in_specs=[smem, hbm],
        out_specs=(smem, hbm),
        scratch_shapes=[
            pltpu.SMEM((2 * n_seq,), i32),
            pltpu.VMEM((tile_rows, features), bf16),
            pltpu.SemaphoreType.DMA,
            pltpu.SemaphoreType.DMA((n_seq,)),
        ],
        compiler_params=pltpu.CompilerParams(vmem_limit_bytes=most_vmem),
        name="place_heads",
    )(head_slot, v2)
    value_main = swap(value_send, seq_axes)

    gains = lax.all_gather(jnp.stack([gain_q, gain_k]), "fsdp", axis=1, tiled=True)
    kq_send, grad_send, extra_send = call(
        functools.partial(norm_kernel, n_seq, heads),
        "normalize",
        [((n_seq, 2, *block), bf16), ((n_seq, *block), bf16), ((extra, 4, *block), bf16)],
        [smem] + [vmem] * 5,
        7 * heads,
        hbm_in=(1, 2, 3, 4),
        hbm_out=(0, 1, 2),
    )(order, q2, k2, v2, g2, gains)
    table = jnp.concatenate([mask_lists, tile_counts[:, :, None]], axis=2)
    table_main = lax.dynamic_index_in_dim(table, order[own], 0, keepdims=False).reshape(-1)
    table_extra = lax.dynamic_index_in_dim(table, order[n_seq + z_index], 0, keepdims=False)
    table_extra = lax.dynamic_index_in_dim(
        table_extra.reshape(n_z, n_x, most + 1), x_index, 1, keepdims=False
    )
    table_extra = jnp.concatenate([table_extra.reshape(-1), x_index[None]])
    extra_own = swap(after(extra_send, (value_main, table_main, table_extra)), "z")

    def attention(parts, name, n_query, at, outs, n_operands, passes, hbm_in=(), hbm_out=()):
        group = 2
        tile_f32 = pltpu.VMEM((n_tiles, *block), f32)
        tile_bf16 = pltpu.VMEM((n_tiles, *block), bf16)
        scratch = {"scores": pltpu.VMEM((group, most, *block), f32)}
        if "forward" in parts:
            scratch |= {"vt": tile_bf16, "dv": tile_f32}
        if "backward" in parts:
            scratch |= {"kt": tile_bf16, "dk": tile_f32, "sums": pltpu.VMEM((2, 8, head_width), f32)}
            scratch["dprobs"] = scratch["scores"]
        if not at["ahead"]:
            scratch = {n: v for n, v in scratch.items() if n not in ("kt", "vt")}
            scratch["kv"] = pltpu.VMEM((n_tiles, 2, *block), bf16)
        at = {**at, "scratch": list(scratch), "results": list(outs)}
        return call(
            functools.partial(attention_kernel, parts, most, n_query, n_tiles, group, at),
            name,
            list(outs.values()),
            [smem] + [vmem] * n_operands,
            10 * n_tiles,
            flops=n_query * most * passes * 2 * tile_rows * tile_rows * head_width,
            scratch=list(scratch.values()),
            hbm_in=hbm_in,
            hbm_out=hbm_out,
        )

    rows_of = lambda n: ((n, tile_rows), f32)

    def shift(values, s):
        return lax.ppermute(values, "x", [(x, (x + s) % n_x) for x in range(n_x)])

    kv_own = extra_own[:, 2:4]
    kv_left, kv_right = shift(kv_own, 1), shift(kv_own, n_x - 1)
    half = n_z // 2
    kv_shifted = [kv_left, shift(kv_left[:half], 1), shift(kv_right[half:], n_x - 1), kv_right]
    grad_main = swap(after(grad_send, extra_own), seq_axes)
    kq_main = swap(after(kq_send, (grad_main, kv_shifted)), seq_axes)
    kv_shifted = after(kv_shifted, grad_main)
    odq_extra, lse_extra, gain_extra, *dkv_parts = attention(
        ("forward", "backward"),
        "attention_second",
        n_z,
        {
            "operands": ["own", "kv1", "kv2", "kv2_rest", "kv3"],
            "key": lambda r, t: r["kv"][t, 0],
            "value": lambda r, t: r["kv"][t, 1],
            "query": lambda r, i: r["own"][i, 0],
            "grad": lambda r, i: r["own"][i, 1],
            "ahead": False,
            "prologue": functools.partial(load_shifted, n_x, n_z),
            "epilogue": functools.partial(store_shifted, n_x, n_z),
            "store_out": setter("odq", lambda i: (i, 0)),
            "store_dq": setter("odq", lambda i: (i, 1)),
            "store_dk": store_part(0),
            "store_dv": store_part(1),
        },
        {
            "odq": ((n_z, 2, *block), bf16),
            "lse": rows_of(n_z),
            "gains": ((2, head_width), f32),
            **{f"part{s}": ((n_z, 2, *block), bf16) for s in range(n_x)},
        },
        n_x + 1,
        20,
    )(table_extra, extra_own, *kv_shifted)
    relayed = shift(dkv_parts[2], n_x - 1)
    (joined,) = call(add_kernel, "add_parts", [((n_z, 2, *block), bf16)], [vmem] * 2, 6 * n_z)(
        dkv_parts[3], relayed
    )
    dkv_parts = [dkv_parts[0], shift(dkv_parts[1], 1), shift(joined, n_x - 1)]
    main_at = {
        "ahead": True,
        "epilogue": functools.partial(every_tile, n_tiles),
        "key": lambda r, t: r["kq"][t, 0],
        "value": lambda r, t: r["v"][t],
        "query": lambda r, i: r["kq"][i, 1],
        "grad": lambda r, i: r["g"][i],
    }
    (extra_back,) = call(
        collect_kernel, "collect", [((n_z, 4, *block), bf16)], [vmem] * 4, 12 * n_z
    )(odq_extra, *dkv_parts)
    extra_home = swap(after(extra_back, kq_main), "z")
    odv_main, lse_main, delta_main = attention(
        ("forward",),
        "forward_first",
        n_tiles,
        {
            **main_at,
            "operands": ["kq", "v", "g"],
            "store_out": setter("odv", lambda i: (i, 0)),
            "store_dv": setter("odv", lambda t: (t, 1)),
        },
        {"odv": ((n_tiles, 2, *block), bf16), "lse": rows_of(n_tiles), "delta": rows_of(n_tiles)},
        3,
        10,
        hbm_in=(1, 2, 3),
        hbm_out=(0,),
    )(table_main, kq_main, value_main, grad_main)
    odv_home = swap(after(odv_main, extra_home), seq_axes)
    dqk_main, gain_main = attention(
        ("backward",),
        "backward_first",
        n_tiles,
        {
            **main_at,
            "operands": ["kq", "v", "g", "lse", "delta"],
            "store_dq": setter("dqk", lambda i: (i, pl.ds(0, tile_rows))),
            "store_dk": store_dk_first,
        },
        {"dqk": ((n_tiles, 2 * tile_rows + shared_rows, head_width), bf16), "gains": ((2, head_width), f32)},
        5,
        16,
        hbm_in=(1, 2, 3),
        hbm_out=(0,),
    )(table_main, kq_main, value_main, grad_main, lse_main, delta_main)

    gain_sums = lax.psum(jnp.concatenate([gain_main, gain_extra]), "fsdp")
    dqk_shape = (n_tiles, 2 * tile_rows + shared_rows, head_width)
    dqk_main = pl.pallas_call(
        share_kernel,
        out_shape=jax.ShapeDtypeStruct(dqk_shape, bf16),
        in_specs=[vmem, vmem, hbm],
        out_specs=hbm,
        input_output_aliases={2: 0},
        scratch_shapes=[
            pltpu.VMEM((shared_rows, head_width), f32),
            pltpu.VMEM((shared_rows, head_width), bf16),
            pltpu.SemaphoreType.DMA((n_seq,)),
        ],
        compiler_params=pltpu.CompilerParams(vmem_limit_bytes=most_vmem),
        name="share_rows",
    )(gain_sums, lse_extra, dqk_main)
    dqk_home = swap(after(dqk_main, odv_home), seq_axes)

    wide = ((tile_rows, features), bf16)
    attn_out, grad_v = call(
        functools.partial(merge_kernel, n_seq, heads),
        "merge_heads",
        [wide, wide],
        [smem, vmem, vmem],
        4 * heads,
        hbm_in=(1, 2),
        hbm_out=(0, 1),
    )(order, odv_home, extra_home)
    per = heads // n_f
    grad_q, grad_k, lse_slots, share_q, share_k = call(
        functools.partial(back_kernel, n_x, n_z, heads, per),
        "gradients_home",
        [
            wide,
            wide,
            ((2, n_tiles * tile_rows), f32),
            ((per, head_width), f32),
            ((per, head_width), f32),
        ],
        [smem] + [vmem] * 5 + [smem] * 2 + [vmem] * 3,
        6 * heads,
        scratch=[
            pltpu.VMEM((n_seq, shared_rows, head_width), f32),
            pltpu.VMEM((2, n_tiles, tile_rows), f32),
        ],
        hbm_in=(2, 1, 3, 4),
        hbm_out=(0, 1),
        lazy=True,
    )(
        order,
        dqk_home,
        extra_home,
        q2,
        k2,
        gains,
        head_slot,
        jnp.stack([own, f_index]),
        lse_main,
        gain_q.reshape(per, head_width),
        gain_k.reshape(per, head_width),
    )
    whole = lambda a: a.reshape(1, tile_rows, features)
    return (
        whole(attn_out),
        lse_slots[None],
        whole(grad_q),
        whole(grad_k),
        whole(grad_v),
        share_q.reshape(-1),
        share_k.reshape(-1),
    )


def solution(mesh):
    n_seq, n_f = mesh.devices.shape
    n_z = 8
    grid = Mesh(mesh.devices.reshape(n_z, n_seq // n_z, n_f), ("z", "x", "fsdp"))
    rows = P("fsdp", ("z", "x"), None)
    in_specs = (rows,) * 4 + (P("fsdp"),) * 2 + (P(),) * 3
    out_specs = (rows,) * 5 + (P("fsdp"),) * 2
    return jax.shard_map(shards, mesh=grid, in_specs=in_specs, out_specs=out_specs, check_vma=False)
```
